32 devices in a mesh: wave: 4 (over z), row: 8 (over y, x, core).
Axes of the slice: x: 2, y: 2, z: 4, core: 2. Of those that a mesh axis runs over, the one named last changes fastest.
Arguments:
- lyot_field: bfloat16 [4, 4096, 2, 4096], P('wave', 'row'), may hold values from -6 to 6
- wave_scale: float32 [4], P('wave'), may hold values from 0.35 to 0.7
- trace_start: int32 [4, 1024, 1024], P(None, 'row', 'wave'), may hold values from -8 to 4102, as said below
- trace_length: int32 [4, 1024, 1024], P(None, 'row', 'wave'), may hold values from 1 to 8, as said below
- column_slot: int32 [1024, 1024], P('row', 'wave'), may hold values from 0 to 3
Outputs:
- detector: float32 [4096, 4096], P('row', 'wave')
The draws below stay inside these ranges and needn't reach their ends.
Inputs may be any that keep to these rules, and one draw needn't show every extreme that they name: trace_start[w, v, u] equals 4 v + w plus an offset between -8 and 7; both ends of the offset are reached. `trace_length`: the value 8 is reached.
All inputs are finite; a program needn't handle non-finite values.
Results may differ from the reference program's by a relative error of at most 0.0031.
Values may be sent and summed in bfloat16 or wider, within the bound.
No kernel may reach another device: no remote copies, remote signals or barrier semaphores. Data moves between devices by JAX's collectives and lax.ppermute only.
A program may use at most 128 MiB of HBM per device.

```python
import math
import jax
import jax.numpy as jnp
from jax import lax

NP = 4096
NQ = 1024
OFFSET = 8
LMAX = 8
WAVES = 4


def draw_trace_start(key, part):
    offsets = jax.random.randint(key, (WAVES, NQ, NQ), -OFFSET, OFFSET, dtype=jnp.int32)
    offsets = offsets.at[0, 0, 0].set(-OFFSET).at[WAVES - 1, NQ - 1, 0].set(OFFSET - 1)
    wave_pos = jnp.arange(WAVES, dtype=jnp.int32)[:, None, None]
    lens_row = jnp.arange(NQ, dtype=jnp.int32)[None, :, None]
    return 4 * lens_row + wave_pos + offsets


def draw_trace_length(key, part):
    lengths = jax.random.randint(jax.random.fold_in(key, 7), (WAVES, NQ, NQ), 1, LMAX + 1, dtype=jnp.int32)
    return lengths.at[0, 0, 0].set(LMAX)


def set_ends(drawn, key, least, top_value):
    shape = drawn.shape
    place = [jax.random.randint(jax.random.fold_in(key, axis), (), 0, shape[axis]) for axis in range(len(shape))]
    drawn = drawn.at[tuple(place)].set(least)
    longest = shape.index(max(shape))
    place[longest] = (place[longest] + 1) % shape[longest]
    return drawn.at[tuple(place)].set(top_value)


def level_of(key, extent, cuts, smallest, high):
    gain, own = 1.0, jax.random.fold_in(key, 6)
    for axis_at, blocks in cuts:
        heights = jnp.exp(jax.random.uniform(jax.random.fold_in(own, axis_at), (blocks,), jnp.float32, smallest / len(cuts), high / len(cuts)))
        gain = gain * jnp.repeat(heights, extent[axis_at] // blocks).reshape([-1 if axis == axis_at else 1 for axis in range(len(extent))])
    return gain


def noise(rng, extent, deviation, limit, pieces=(), held_as=jnp.bfloat16):
    array = jax.random.normal(rng, extent, jnp.float32) * deviation
    if len(pieces) > 0:
        array = level_of(rng, extent, pieces, -0.22, 0.18) * array
    return jnp.clip(array, min=-limit, max=limit).astype(held_as)


def setup_inputs(seed: int = 0) -> dict:
    arg_keys = jax.random.split(jax.random.key(seed), 6)
    lyot_field = noise(arg_keys[0], (WAVES, NP, 2, NP), 1.0, 6.0, ((0, 4), (1, 8)))
    wave_scale = jnp.clip(jnp.exp(math.log(0.7) - 0.6931472 * jax.random.uniform(arg_keys[1], (WAVES,), jnp.float32) ** level_of(arg_keys[1], (WAVES,), ((0, 4),), -0.2, 0.2)), 0.35, 0.7)
    trace_start = draw_trace_start(jax.random.fold_in(arg_keys[5], 71), 0)
    trace_length = draw_trace_length(jax.random.fold_in(arg_keys[5], 71), 0)
    column_slot = set_ends(jax.random.randint(arg_keys[4], (NQ, NQ), 0, 4), jax.random.fold_in(arg_keys[4], 1), 0, 3).astype(jnp.int32)
    return dict(lyot_field=lyot_field, wave_scale=wave_scale, trace_start=trace_start, trace_length=trace_length, column_slot=column_slot)


def mft_parts(scale):
    pupil_pos = jnp.arange(NP, dtype=jnp.float32) - (NP - 1) / 2.0
    lens_pos = jnp.arange(NQ, dtype=jnp.float32) - (NQ - 1) / 2.0
    phase = pupil_pos[:, None] * lens_pos[None, :] * (scale * (2.0 * math.pi / NP))
    norm = 1.0 / math.sqrt(NP)
    table_real = (jnp.cos(phase) * norm).astype(jnp.bfloat16)
    table_imag = (-jnp.sin(phase) * norm).astype(jnp.bfloat16)
    return (table_real, table_imag)

def intensity_of(pair):
    field, scale = pair
    table_real, table_imag = mft_parts(scale)
    real_part = field[:, 0, :]
    imag_part = field[:, 1, :]
    half_real = jnp.dot(real_part, table_real, preferred_element_type=jnp.float32) - jnp.dot(imag_part, table_imag, preferred_element_type=jnp.float32)
    half_imag = jnp.dot(real_part, table_imag, preferred_element_type=jnp.float32) + jnp.dot(imag_part, table_real, preferred_element_type=jnp.float32)
    half_real = half_real.astype(jnp.bfloat16)
    half_imag = half_imag.astype(jnp.bfloat16)
    lens_real = jnp.dot(half_real.T, table_real, preferred_element_type=jnp.float32) - jnp.dot(half_imag.T, table_imag, preferred_element_type=jnp.float32)
    lens_imag = jnp.dot(half_real.T, table_imag, preferred_element_type=jnp.float32) + jnp.dot(half_imag.T, table_real, preferred_element_type=jnp.float32)
    return lens_real * lens_real + lens_imag * lens_imag

def reference(lyot_field, wave_scale, trace_start, trace_length, column_slot):
    intensity = lax.map(intensity_of, (lyot_field, wave_scale))
    waves_all = lyot_field.shape[0]
    padding = OFFSET + waves_all + LMAX
    detector_cols = 4 * NQ
    total_rows = 4 * NQ + 2 * padding
    deposit = intensity / trace_length.astype(jnp.float32)
    column = 4 * jnp.arange(NQ, dtype=jnp.int32)[None, :] + column_slot
    column = jnp.broadcast_to(column[None, :, :], trace_start.shape)
    top_row = trace_start + padding
    bottom_row = top_row + trace_length
    edges = jnp.zeros((total_rows * detector_cols,), jnp.float32)
    edges = edges.at[(top_row * detector_cols + column).ravel()].add(deposit.ravel())
    edges = edges.at[(bottom_row * detector_cols + column).ravel()].add(-deposit.ravel())
    image = jnp.cumsum(edges.reshape(total_rows, detector_cols), axis=0)
    return image[padding:padding + 4 * NQ]
```

```python
import functools
import math

import jax
import jax.numpy as jnp
from jax import lax
from jax.experimental import pallas as pl
from jax.experimental.pallas import tpu as pltpu
from jax.sharding import PartitionSpec as P

NQ = 1024
OFFSET = 8
LMAX = 8
LANES = 128
F32 = jnp.float32
BF16 = jnp.bfloat16
VMEM_LIMIT = 48 * 1024 * 1024


def iota(shape, dim):
    return lax.broadcasted_iota(jnp.int32, shape, dim)


def dot_nt(a, b):
    return lax.dot_general(a, b, (((1,), (1,)), ((), ())), preferred_element_type=F32)


def one_hot(mask):
    return jnp.where(mask, 1.0, 0.0).astype(BF16)


def cos_sin_turns(turns):
    angle = (turns - jnp.round(turns)) * math.pi
    square = angle * angle
    sine = jnp.full_like(angle, 1.0 / math.factorial(13))
    for order in (11, 9, 7, 5, 3, 1):
        sine = sine * square + (-1.0) ** ((order - 1) // 2) / math.factorial(order)
    sine = sine * angle
    cosine = jnp.full_like(angle, 1.0 / math.factorial(16))
    for order in (14, 12, 10, 8, 6, 4, 2, 0):
        cosine = cosine * square + (-1.0) ** (order // 2) / math.factorial(order)
    return 1.0 - 2.0 * sine * sine, 2.0 * sine * cosine


def chunk_rows(block, edge):
    if edge == 0 or 2 * edge >= block:
        return [[(0, block)]]
    return [[(0, edge), (block - edge, block)], [(edge, block - edge)]]


def count_of(ranges):
    return sum(stop - start for start, stop in ranges)


def half_kernel(ranges, parts, block, pupil, me_ref, scale_ref, field_ref, *rest):
    outs, table_ref = rest[:parts], rest[parts]
    total, turn, step, halves = rest[parts + 1 :]
    index = pl.program_id(0)
    rows_total = total.shape[0]
    half = rows_total // 2
    rows = count_of(ranges)
    width = table_ref.shape[1]
    samples = field_ref.shape[0]

    @pl.when(index == 0)
    def start():
        scale = scale_ref[0]
        coarse = jnp.floor(scale * 4096.0) * (1.0 / 4096.0)
        fine = scale - coarse
        for group in range(parts // 2):
            at = group * rows
            for low, high in ranges:
                shape = (high - low, LANES)
                lens = (iota(shape, 0) + (group * block + low)).astype(F32) - (NQ - 1) / 2.0
                place = iota(shape, 1).astype(F32) - (pupil - 1) / 2.0
                cosine, sine = cos_sin_turns(lens * place * (scale * (1.0 / pupil)))
                norm = 1.0 / math.sqrt(pupil)
                here = slice(at, at + high - low)
                turn[0, here] = cosine * norm
                turn[1, here] = sine * norm
                whole = lens * coarse * (LANES / pupil)
                whole = whole - jnp.round(whole)
                cosine, sine = cos_sin_turns(whole + lens * fine * (LANES / pupil))
                step[0, here] = cosine
                step[1, here] = sine
                at += high - low

    for piece in range(width // LANES):
        cosine, sine = turn[0], turn[1]
        lanes = slice(piece * LANES, (piece + 1) * LANES)
        table_ref[:half, lanes] = cosine.astype(BF16)
        table_ref[half:, lanes] = sine.astype(BF16)
        turn[0] = cosine * step[0] - sine * step[1]
        turn[1] = sine * step[0] + cosine * step[1]
    field = field_ref[...].reshape(2 * samples, width)
    product = dot_nt(table_ref[...], field)

    @pl.when(index == 0)
    def first():
        total[...] = product

    @pl.when(index > 0)
    def later():
        total[...] += product

    @pl.when(index == pl.num_programs(0) - 1)
    def finish():
        me = me_ref[0]
        source, target = iota((2 * LANES, 2 * LANES), 0), iota((2 * LANES, 2 * LANES), 1)
        apart = one_hot(
            source == jnp.where(target < LANES, 2 * target, 2 * (target - LANES) + 1)
        )
        for piece in range(samples // LANES):
            even_odd = []
            for side in range(2):
                lanes = slice((2 * piece + side) * LANES, (2 * piece + side + 1) * LANES)
                direct, cross = total[:half, lanes], total[half:, lanes]
                real_lane = iota(cross.shape, 1) % 2 == 0
                swapped = jnp.where(
                    real_lane, pltpu.roll(cross, LANES - 1, 1), -pltpu.roll(cross, 1, 1)
                )
                even_odd.append((direct + swapped, direct - swapped))
            lanes = slice(piece * LANES, (piece + 1) * LANES)
            for mirrored in range(2):
                both = jnp.concatenate([pair[mirrored] for pair in even_odd], axis=1)
                both = jnp.dot(both.astype(BF16), apart, preferred_element_type=F32).astype(BF16)
                for group in range(parts // 2):
                    owner = parts - 1 - group if mirrored else group
                    here = slice(group * rows, (group + 1) * rows)
                    halves[owner, 0, :, lanes] = both[here, :LANES]
                    halves[owner, 1, :, lanes] = both[here, LANES:]
        for hop in range(parts):
            outs[hop][...] = halves[me ^ hop]


def half_transform(ranges, parts, block, me, scale, field):
    samples, _, pupil = field.shape
    rows = count_of(ranges)
    height = parts * rows
    width = min(1024, pupil)
    grid_spec = pltpu.PrefetchScalarGridSpec(
        num_scalar_prefetch=2,
        grid=(pupil // width,),
        in_specs=[pl.BlockSpec((samples, 2, width), lambda i, me, scale: (0, 0, i))],
        out_specs=[pl.BlockSpec((2, rows, samples), lambda i, me, scale: (0, 0, 0))] * parts
        + [pl.BlockSpec((height, width), lambda i, me, scale: (0, i))],
        scratch_shapes=[
            pltpu.VMEM((height, 2 * samples), F32),
            pltpu.VMEM((2, height // 2, LANES), F32),
            pltpu.VMEM((2, height // 2, LANES), F32),
            pltpu.VMEM((parts, 2, rows, samples), BF16),
        ],
    )
    results = pl.pallas_call(
        functools.partial(half_kernel, ranges, parts, block, pupil),
        grid_spec=grid_spec,
        out_shape=[jax.ShapeDtypeStruct((2, rows, samples), BF16)] * parts
        + [jax.ShapeDtypeStruct((height, pupil), BF16)],
        compiler_params=pltpu.CompilerParams(vmem_limit_bytes=VMEM_LIMIT),
        cost_estimate=pl.CostEstimate(
            flops=4 * height * samples * pupil,
            bytes_accessed=2 * (2 * samples * pupil + height * pupil),
            transcendentals=0,
        ),
        name="half_transform",
    )(me, scale, field)
    return results[:parts], results[parts]


def lens_kernel(layout, parts, waves, block, me_ref, wave_ref, *rest):
    tables, rest = rest[: len(layout)], rest[len(layout) :]
    pieces, rest = rest[:parts], rest[parts:]
    outs, totals, tiles = rest[:waves], rest[waves : waves + len(layout)], rest[-1]
    index = pl.program_id(0)
    rows = pieces[0].shape[1]
    samples = pieces[0].shape[2]

    for hop in range(parts):

        @pl.when(index == hop)
        def add(hop=hop):
            piece = pieces[hop][...].reshape(2 * rows, samples)
            for table, total in zip(tables, totals):
                product = dot_nt(table[...], piece)
                if hop == 0:
                    total[...] = product
                else:
                    total[...] += product

    @pl.when(index == parts - 1)
    def finish():
        flip = me_ref[0] >= parts // 2
        shape = (rows, 2 * rows)
        wanted = jnp.where(flip, rows - 1 - iota(shape, 0), iota(shape, 0))
        pick = one_hot(iota(shape, 1) == wanted)
        columns = tiles.shape[2]
        per_tile = columns // block
        back = one_hot(
            iota((columns, columns), 0) == columns - 1 - iota((columns, columns), 1)
        )
        across = {}
        for ranges, total in zip(layout, totals):
            half = total.shape[0] // 2
            direct, cross = total[:half], total[half:]
            swapped = pltpu.roll(cross, rows, 1)
            swapped = jnp.where(iota(cross.shape, 1) < rows, swapped, -swapped)
            for mirrored in range(2):
                value = direct - swapped if mirrored else direct + swapped
                value = value * value
                value = value + pltpu.roll(value, rows, 1)
                across[ranges, mirrored] = value.astype(BF16)
        for group in range(waves // 2):
            for mirrored in range(2):
                strips = []
                for part in range(group * per_tile, (group + 1) * per_tile):
                    spans = []
                    for ranges in layout:
                        at = part * count_of(ranges)
                        for low, high in ranges:
                            spans.append((low, ranges, at, at + high - low))
                            at += high - low
                    for _, ranges, start, stop in sorted(spans):
                        strips.append(across[ranges, mirrored][start:stop])
                strip = jnp.concatenate(strips, axis=0)
                turned = dot_nt(pick, strip).astype(BF16)
                if mirrored:
                    turned = jnp.dot(turned, back, preferred_element_type=F32).astype(BF16)
                tiles[waves - 1 - group if mirrored else group] = turned
        for hop in range(waves):
            outs[hop][...] = tiles[wave_ref[0] ^ hop]


def lens_intensity(layout, parts, waves, block, me, wave, tables, pieces):
    _, rows, samples = pieces[0].shape
    columns = NQ // waves
    heights = [table.shape[0] for table in tables]

    def whole(i, me, wave):
        return (0, 0, 0)

    grid_spec = pltpu.PrefetchScalarGridSpec(
        num_scalar_prefetch=2,
        grid=(parts,),
        in_specs=[
            pl.BlockSpec((height, samples), lambda i, me, wave: (0, me[0] ^ i))
            for height in heights
        ]
        + [pl.BlockSpec((2, rows, samples), whole)] * parts,
        out_specs=[pl.BlockSpec((rows, columns), lambda i, me, wave: (0, 0))] * waves,
        scratch_shapes=[pltpu.VMEM((height, 2 * rows), F32) for height in heights]
        + [pltpu.VMEM((waves, rows, columns), BF16)],
    )
    return pl.pallas_call(
        functools.partial(lens_kernel, layout, parts, waves, block),
        grid_spec=grid_spec,
        out_shape=[jax.ShapeDtypeStruct((rows, columns), BF16)] * waves,
        compiler_params=pltpu.CompilerParams(vmem_limit_bytes=VMEM_LIMIT),
        cost_estimate=pl.CostEstimate(
            flops=4 * rows * sum(heights) * samples * parts,
            bytes_accessed=2 * sum(heights) * samples * parts,
            transcendentals=0,
        ),
        name="lens_intensity",
    )(me, wave, *tables, *pieces)


def shifts(waves):
    return -(OFFSET // 4), (waves - 1 + OFFSET - 1 + LMAX - 1) // 4


def block_light(amounts, masks, slots, at, waves, reach):
    light = [[None] * 4 for _ in range(4)]
    near = pl.ds(at, 24)
    slots_near = slots[near]
    values_near = [amounts[wave, near] for wave in range(waves)]
    masks_near = [masks[wave, near] for wave in range(waves)]
    for shift in range(reach[0], reach[1] + 1):
        rows = slice(8 - shift, 16 - shift)
        slot = slots_near[rows]
        value = [held[rows] for held in values_near]
        mask = [held[rows] for held in masks_near]
        picks = [slot == which for which in range(4)]
        for step in range(4):
            height = 4 * shift + step
            strip = None
            for wave in range(waves):
                if not wave - OFFSET <= height <= wave + OFFSET + LMAX - 2:
                    continue
                bit = (mask[wave] & (1 << (height + OFFSET))) != 0
                term = jnp.where(bit, value[wave], 0.0)
                strip = term if strip is None else strip + term
            if strip is None:
                continue
            for which in range(4):
                term = jnp.where(picks[which], strip, 0.0)
                held = light[step][which]
                light[step][which] = term if held is None else held + term
    return light


def stage_tile(amounts, masks, slots, wave, hop, tile, starts, lengths, slot, first, here, rows):
    which = wave ^ hop
    span = (tile.shape[0], tile.shape[1])
    length = lengths[which, rows]
    place = starts[which, rows] - 4 * (first + iota(span, 0))
    amounts[which, here] = tile.astype(F32) / length.astype(F32)
    masks[which, here] = ((1 << length) - 1) << (place + OFFSET)


def put_planes(light, planes, at):
    for step in range(4):
        for which in range(4):
            value = light[step][which]
            for part in range(value.shape[1] // LANES):
                lanes = slice(part * LANES, (part + 1) * LANES)
                planes.at[4 * part + which][pl.Slice(at + step, 8, 4), :] = value[:, lanes]


def spread(planes, out_ref, rows):
    source, target = iota((2 * LANES, 4 * LANES), 0), iota((2 * LANES, 4 * LANES), 1)
    for part in range(planes.shape[0] // 4):
        value = None
        for pair in range(2):
            slot = 2 * pair + source // LANES
            place = one_hot(target == 4 * (source % LANES) + slot)
            at = 4 * part + 2 * pair
            plane = jnp.concatenate([planes[at, rows], planes[at + 1, rows]], axis=1)
            high = plane.astype(BF16)
            low = (plane - high.astype(F32)).astype(BF16)
            term = jnp.dot(high, place, preferred_element_type=F32)
            term = term + jnp.dot(low, place, preferred_element_type=F32)
            value = term if value is None else value + term
        out_ref[rows, part * 4 * LANES : (part + 1) * 4 * LANES] = value


def edge_kernel(ranges, waves, place_ref, *rest):
    tiles, rest = rest[:waves], rest[waves:]
    starts, lengths, slot, up_ref, down_ref, amounts, masks, slots, planes = rest
    block, columns = slot.shape
    lens0 = place_ref[0] * block
    wave = place_ref[1]
    amounts[...] = jnp.zeros_like(amounts)
    masks[...] = jnp.zeros_like(masks)
    slots[...] = jnp.zeros_like(slots)
    rows_in = count_of(ranges)
    for side, out_ref in enumerate((up_ref, down_ref)):
        rows = slice(block - 8, block) if side else slice(0, 8)
        held = slice(rows_in - 8, rows_in) if side else slice(0, 8)
        first = lens0 + rows.start
        here = slice(16, 24)
        for hop in range(waves):
            tile = tiles[hop][...].astype(F32)[held]
            stage_tile(amounts, masks, slots, wave, hop, tile, starts, lengths, slot, first, here, rows)
        slots[here] = slot[rows]
        low, high = shifts(waves)
        at, reach = (16, (1, high)) if side else (0, (low, -1))
        light = block_light(amounts, masks, slots, at, waves, reach)
        put_planes(light, planes, 0)
        spread(planes, out_ref, slice(0, 32))


def edge_light(ranges, waves, place, tiles, starts, lengths, slot):
    block, columns = slot.shape
    return pl.pallas_call(
        functools.partial(edge_kernel, ranges, waves),
        in_specs=[pl.BlockSpec(memory_space=pltpu.SMEM)]
        + [pl.BlockSpec(memory_space=pltpu.VMEM)] * (waves + 3),
        out_specs=[pl.BlockSpec(memory_space=pltpu.VMEM)] * 2,
        out_shape=[jax.ShapeDtypeStruct((32, 4 * columns), F32)] * 2,
        scratch_shapes=[
            pltpu.VMEM((waves, 40, columns), F32),
            pltpu.VMEM((waves, 40, columns), jnp.int32),
            pltpu.VMEM((40, columns), jnp.int32),
            pltpu.VMEM((4 * columns // LANES, 32, LANES), F32),
        ],
        compiler_params=pltpu.CompilerParams(vmem_limit_bytes=VMEM_LIMIT),
        name="edge_light",
    )(place, *tiles, starts, lengths, slot)


def tile_kernel(layout, waves, place_ref, *rest):
    tiles, rest = rest[: waves * len(layout)], rest[waves * len(layout) :]
    starts, lengths, slot, above, below, out_ref, amounts, masks, slots, planes = rest
    block, columns = slot.shape
    lens0 = place_ref[0] * block
    wave = place_ref[1]
    for edge in (slice(0, 8), slice(block + 8, block + 16)):
        amounts[:, edge] = jnp.zeros((waves, 8, columns), F32)
        masks[:, edge] = jnp.zeros((waves, 8, columns), jnp.int32)
        slots[edge] = jnp.zeros((8, columns), jnp.int32)
    slots[8 : block + 8] = slot[...]
    for part, ranges in enumerate(layout):
        for hop in range(waves):
            at = 0
            for low, high in ranges:
                tile = tiles[part * waves + hop][at : at + high - low].astype(F32)
                at += high - low
                stage_tile(
                    amounts, masks, slots, wave, hop, tile, starts, lengths, slot,
                    lens0 + low, slice(low + 8, high + 8), slice(low, high),
                )

    def body(group, _):
        at = pl.multiple_of(group * 8, 8)
        light = block_light(amounts, masks, slots, at, waves, shifts(waves))
        put_planes(light, planes, at * 4)
        return 0

    lax.fori_loop(0, block // 8, body, 0)
    spread(planes, out_ref, slice(0, 4 * block))
    out_ref[:32] += above[...]
    out_ref[4 * block - 32 :] += below[...]


def tile_light(layout, waves, place, tiles, starts, lengths, slot, above, below):
    block, columns = slot.shape
    return pl.pallas_call(
        functools.partial(tile_kernel, layout, waves),
        in_specs=[pl.BlockSpec(memory_space=pltpu.SMEM)]
        + [pl.BlockSpec(memory_space=pltpu.VMEM)] * (len(tiles) + 5),
        out_specs=pl.BlockSpec(memory_space=pltpu.VMEM),
        out_shape=jax.ShapeDtypeStruct((4 * block, 4 * columns), F32),
        scratch_shapes=[
            pltpu.VMEM((waves, block + 16, columns), F32),
            pltpu.VMEM((waves, block + 16, columns), jnp.int32),
            pltpu.VMEM((block + 16, columns), jnp.int32),
            pltpu.VMEM((4 * columns // LANES, 4 * block, LANES), F32),
        ],
        compiler_params=pltpu.CompilerParams(vmem_limit_bytes=VMEM_LIMIT),
        name="tile_light",
    )(place, *tiles, starts, lengths, slot, above, below)


def exchange(pieces, axis):
    count = lax.axis_size(axis)
    return [pieces[0]] + [
        lax.ppermute(pieces[hop], axis, [(source, source ^ hop) for source in range(count)])
        for hop in range(1, count)
    ]


def shifted(value, axis, steps):
    count = lax.axis_size(axis)
    initial, last = (max(0, -steps), min(count, count - steps))
    return lax.ppermute(value, axis, [(source, source + steps) for source in range(initial, last)])


def per_device(lyot_field, wave_scale, trace_start, trace_length, column_slot):
    parts, waves = lax.axis_size("row"), lax.axis_size("wave")
    block = column_slot.shape[0]
    row_index = lax.axis_index("row").astype(jnp.int32)
    wave_index = lax.axis_index("wave").astype(jnp.int32)
    me, wave = row_index.reshape(1), wave_index.reshape(1)
    place = jnp.stack([row_index, wave_index])
    layout = tuple(tuple(ranges) for ranges in chunk_rows(block, EDGE * block // 128))
    sent, tables = [], []
    for ranges in layout:
        pieces, table = half_transform(ranges, parts, block, me, wave_scale, lyot_field[0])
        sent.append(exchange(pieces, "row"))
        tables.append(table)
    tiles = []
    for pieces in sent:
        intensity = lens_intensity(layout, parts, waves, block, me, wave, tables, pieces)
        tiles.append(exchange(intensity, "wave"))
    up, down = edge_light(layout[0], waves, place, tiles[0], trace_start, trace_length, column_slot)
    above = shifted(down, "row", 1)
    below = shifted(up, "row", -1)
    return tile_light(
        layout, waves, place, [tile for part in tiles for tile in part],
        trace_start, trace_length, column_slot, above, below,
    )


EDGE = 32


def solution(mesh):
    placed = (
        P("wave", "row", None, None),
        P("wave"),
        P(None, "row", "wave"),
        P(None, "row", "wave"),
        P("row", "wave"),
    )
    return jax.shard_map(
        per_device, mesh=mesh, in_specs=placed, out_specs=P("row", "wave"), check_vma=False
    )
```

```python
import functools
import math

import jax
import jax.numpy as jnp
from jax import lax
from jax.experimental import pallas as pl
from jax.experimental.pallas import tpu as pltpu
from jax.sharding import PartitionSpec as P

NQ = 1024
OFFSET = 8
LMAX = 8
LANES = 128
F32 = jnp.float32
BF16 = jnp.bfloat16
MIB = 1024 * 1024
VMEM_LIMIT = 20 * MIB


def iota(shape, dim):
    return lax.broadcasted_iota(jnp.int32, shape, dim)


def dot_nt(a, b):
    return lax.dot_general(a, b, (((1,), (1,)), ((), ())), preferred_element_type=F32)


def one_hot(mask):
    return jnp.where(mask, 1.0, 0.0).astype(BF16)


def cos_sin_turns(turns):
    angle = (turns - jnp.round(turns)) * math.pi
    square = angle * angle
    sine = jnp.full_like(angle, 1.0 / math.factorial(13))
    for order in (11, 9, 7, 5, 3, 1):
        sine = sine * square + (-1.0) ** ((order - 1) // 2) / math.factorial(order)
    sine = sine * angle
    cosine = jnp.full_like(angle, 1.0 / math.factorial(16))
    for order in (14, 12, 10, 8, 6, 4, 2, 0):
        cosine = cosine * square + (-1.0) ** (order // 2) / math.factorial(order)
    return 1.0 - 2.0 * sine * sine, 2.0 * sine * cosine


def chunk_rows(block, halo):
    edge = block // 4 - halo
    return (((-halo, edge), (block - edge, block + halo)), ((edge, block - edge),))


def count_of(ranges):
    return sum(stop - start for start, stop in ranges)


def start_turns(first, here, pupil, scale, turn, step):
    coarse = jnp.floor(scale * 4096.0) * (1.0 / 4096.0)
    fine = scale - coarse
    shape = (here.stop - here.start, LANES)
    lens = (iota(shape, 0) + first).astype(F32) - (NQ - 1) / 2.0
    place = iota(shape, 1).astype(F32) - (pupil - 1) / 2.0
    cosine, sine = cos_sin_turns(lens * place * (scale * (1.0 / pupil)))
    norm = 1.0 / math.sqrt(pupil)
    turn[0, here] = cosine * norm
    turn[1, here] = sine * norm
    whole = lens * coarse * (LANES / pupil)
    whole = whole - jnp.round(whole)
    cosine, sine = cos_sin_turns(whole + lens * fine * (LANES / pupil))
    step[0, here] = cosine
    step[1, here] = sine


def turn_table(low, high, turn, step, table):
    half = table.shape[0] // 2

    for start in range(low, high, LANES):
        cosine, sine = turn[0], turn[1]
        table[:half, start : start + LANES] = cosine.astype(BF16)
        table[half:, start : start + LANES] = sine.astype(BF16)
        turn[0] = cosine * step[0] - sine * step[1]
        turn[1] = sine * step[0] + cosine * step[1]


def table_kernel(scale_ref, *rest):
    table, turn, step = rest[-3:]
    half, pupil = table.shape[0] // 2, table.shape[1]
    for low in range(0, half, 64):
        here = slice(low, min(low + 64, half))
        start_turns(low, here, pupil, scale_ref[0], turn, step)
        rotation = step[0, here], step[1, here]
        cosine, sine = turn[0, here], turn[1, here]
        for start in range(0, pupil, LANES):
            table[here, start : start + LANES] = cosine.astype(BF16)
            table[half + low : half + here.stop, start : start + LANES] = sine.astype(BF16)
            cosine, sine = (
                cosine * rotation[0] - sine * rotation[1],
                sine * rotation[0] + cosine * rotation[1],
            )


def lens_table(scale, pupil, later):
    return pl.pallas_call(
        table_kernel,
        in_specs=[pl.BlockSpec(memory_space=pltpu.SMEM)]
        + [pl.BlockSpec(memory_space=pl.ANY)] * len(later),
        out_specs=pl.BlockSpec(memory_space=pltpu.VMEM),
        out_shape=jax.ShapeDtypeStruct((NQ, pupil), BF16),
        scratch_shapes=[pltpu.VMEM((2, NQ // 2, LANES), F32)] * 2,
        compiler_params=pltpu.CompilerParams(vmem_limit_bytes=VMEM_LIMIT),
        cost_estimate=pl.CostEstimate(flops=1, bytes_accessed=1, transcendentals=0),
        name="lens_table",
    )(scale, *later)


def half_kernel(ranges, parts, block, width, size, extra, me_ref, scale_ref, field_hbm, *rest):
    outs = rest[extra : extra + parts]
    field, table, turn, step, halves, arrived = rest[extra + parts :]
    samples, _, pupil = field_hbm.shape
    half = table.shape[0] // 2
    rows = count_of(ranges)
    loads = {}
    for piece in range(samples // size):
        for low in range(0, pupil, width):
            here = (pl.ds(piece * size, size), slice(None), pl.ds(low, width))
            loads[piece, low] = pltpu.make_async_copy(
                field_hbm.at[here], field.at[here], arrived.at[len(loads)]
            )
            loads[piece, low].start()

    at = 0
    for group in range(parts // 2):
        for low, high in ranges:
            here = slice(at, at + high - low)
            start_turns(group * block + low, here, pupil, scale_ref[0], turn, step)
            at += high - low
    source, target = iota((2 * LANES, 2 * LANES), 0), iota((2 * LANES, 2 * LANES), 1)
    apart = one_hot(source == jnp.where(target < LANES, 2 * target, 2 * (target - LANES) + 1))
    for piece in range(samples // size):
        product = None
        for low in range(0, pupil, width):
            lanes = slice(low, low + width)
            if piece == 0:
                turn_table(low, low + width, turn, step, table)
            loads[piece, low].wait()
            here = field[piece * size : (piece + 1) * size, :, lanes].reshape(2 * size, width)
            term = dot_nt(table[:, lanes], here)
            product = term if product is None else product + term
        for inner in range(size // LANES):
            even_odd = []
            for side in range(2):
                lanes = slice((2 * inner + side) * LANES, (2 * inner + side + 1) * LANES)
                direct, cross = product[:half, lanes], product[half:, lanes]
                swapped = jnp.where(
                    iota(cross.shape, 1) % 2 == 0,
                    pltpu.roll(cross, LANES - 1, 1),
                    -pltpu.roll(cross, 1, 1),
                )
                even_odd.append((direct + swapped, direct - swapped))
            first = piece * size + inner * LANES
            lanes = slice(first, first + LANES)
            for mirrored in range(2):
                both = jnp.concatenate([pair[mirrored] for pair in even_odd], axis=1)
                both = jnp.dot(both.astype(BF16), apart, preferred_element_type=F32)
                for group in range(parts // 2):
                    owner = parts - 1 - group if mirrored else group
                    here = slice(group * rows, (group + 1) * rows)
                    halves[owner, :rows, lanes] = both[here, :LANES].astype(BF16)
                    halves[owner, rows:, lanes] = both[here, LANES:].astype(BF16)
    for hop in range(parts):
        outs[hop][...] = halves[me_ref[0] ^ hop]


def half_transform(ranges, parts, block, me, scale, field, later):
    samples, _, pupil = field.shape
    rows = count_of(ranges)
    height = parts * rows
    width, size = min(WIDTH, pupil), min(SIZE, samples)
    return pl.pallas_call(
        functools.partial(half_kernel, ranges, parts, block, width, size, len(later)),
        in_specs=[pl.BlockSpec(memory_space=pltpu.SMEM)] * 2
        + [pl.BlockSpec(memory_space=pl.ANY)] * (1 + len(later)),
        out_specs=[pl.BlockSpec(memory_space=pltpu.VMEM)] * parts,
        scratch_shapes=[
            pltpu.VMEM(field.shape, BF16),
            pltpu.VMEM((height, pupil), BF16),
            pltpu.VMEM((2, height // 2, LANES), F32),
            pltpu.VMEM((2, height // 2, LANES), F32),
            pltpu.VMEM((parts, 2 * rows, samples), BF16),
            pltpu.SemaphoreType.DMA((pupil // width * (samples // size),)),
        ],
        out_shape=[jax.ShapeDtypeStruct((2 * rows, samples), BF16)] * parts,
        compiler_params=pltpu.CompilerParams(vmem_limit_bytes=ROOM * MIB),
        cost_estimate=pl.CostEstimate(flops=1, bytes_accessed=1, transcendentals=0),
        name="half_transform",
    )(me, scale, field, *later)


def lens_kernel(layout, parts, waves, block, me_ref, wave_ref, table, *rest):
    kinds = len(layout)
    pieces, rest = rest[: kinds * parts], rest[kinds * parts :]
    outs, tiles = rest[:waves], rest[waves]
    me, wave = me_ref[0], wave_ref[0]
    half = table.shape[0] // 2
    samples = pieces[0].shape[1]
    total = None
    for hop in range(parts):
        near = [pieces[kind * parts + hop][...] for kind in range(kinds)]
        lanes = pl.ds(pl.multiple_of((me ^ hop) * samples, samples), samples)
        term = dot_nt(jnp.concatenate(near, axis=0), table[:, lanes])
        total = term if hop == 0 else total + term

    strips, spans, at = ([], []), [], 0
    for ranges in layout:
        rows = count_of(ranges)
        real, imag = total[at : at + rows], total[at + rows : at + 2 * rows]
        at += 2 * rows
        for mirrored, sign in enumerate((1.0, -1.0)):
            lens_real = real[:, :half] + sign * imag[:, half:]
            lens_imag = imag[:, :half] - sign * real[:, half:]
            strips[mirrored].append(lens_real * lens_real + lens_imag * lens_imag)
        spans.extend(ranges)
    height, columns = tiles.shape[1:]
    count = sum(count_of(ranges) for ranges in layout)
    held = iota((height, count), 1)
    row, at = jnp.zeros((height, count), jnp.int32), 0
    for low, high in spans:
        row = jnp.where(held >= at, held - at + low, row)
        at += high - low
    row = jnp.where(me >= parts // 2, block - 1 - row, row)
    pick = one_hot(row == iota((height, count), 0) - MARGIN)
    back = one_hot(iota((columns, columns), 0) == columns - 1 - iota((columns, columns), 1))
    for mirrored in range(2):
        strip = jnp.concatenate(strips[mirrored], axis=0).astype(BF16)
        strip = jnp.dot(pick, strip, preferred_element_type=F32).astype(BF16)
        for group in range(waves // 2):
            tile = strip[:, group * columns : (group + 1) * columns]
            if mirrored:
                tile = jnp.dot(tile, back, preferred_element_type=F32).astype(BF16)
            tiles[waves - 1 - group if mirrored else group] = tile
    for hop in range(waves):
        outs[hop][...] = tiles[wave ^ hop]


def lens_intensity(layout, parts, waves, block, me, wave, table, sent):
    shape = (block + 2 * MARGIN, NQ // waves)
    pieces = [piece for part in sent for piece in part]
    return pl.pallas_call(
        functools.partial(lens_kernel, layout, parts, waves, block),
        in_specs=[pl.BlockSpec(memory_space=pltpu.SMEM)] * 2
        + [pl.BlockSpec(memory_space=pltpu.VMEM)] * (1 + len(pieces)),
        out_specs=[pl.BlockSpec(memory_space=pltpu.VMEM)] * waves,
        out_shape=[jax.ShapeDtypeStruct(shape, BF16)] * waves,
        scratch_shapes=[pltpu.VMEM((waves, *shape), BF16)],
        compiler_params=pltpu.CompilerParams(vmem_limit_bytes=VMEM_LIMIT),
        cost_estimate=pl.CostEstimate(flops=1, bytes_accessed=1, transcendentals=0),
        name="lens_intensity",
    )(me, wave, table, *pieces)


def shifts(waves):
    return -(OFFSET // 4), (waves - 1 + OFFSET - 1 + LMAX - 1) // 4


def block_light(amounts, masks, slots, at, waves, reach):
    light = [[None] * 4 for _ in range(4)]
    near = pl.ds(at, 24)
    slots_near = slots[near]
    values_near = [amounts[wave, near] for wave in range(waves)]
    masks_near = [masks[wave, near] for wave in range(waves)]
    for shift in range(reach[0], reach[1] + 1):
        rows = slice(8 - shift, 16 - shift)
        slot = slots_near[rows]
        value = [held[rows] for held in values_near]
        mask = [held[rows] for held in masks_near]
        picks = [slot == which for which in range(4)]
        for step in range(4):
            height = 4 * shift + step
            strip = None
            for wave in range(waves):
                if not wave - OFFSET <= height <= wave + OFFSET + LMAX - 2:
                    continue
                bit = (mask[wave] & (1 << (height + OFFSET))) != 0
                term = jnp.where(bit, value[wave], 0.0)
                strip = term if strip is None else strip + term
            if strip is None:
                continue
            for which in range(4):
                term = jnp.where(picks[which], strip, 0.0)
                held = light[step][which]
                light[step][which] = term if held is None else held + term
    return light


def put_planes(light, planes, at):
    for step in range(4):
        for which in range(4):
            value = light[step][which]
            for part in range(value.shape[1] // LANES):
                lanes = slice(part * LANES, (part + 1) * LANES)
                planes.at[4 * part + which][pl.Slice(at + step, 8, 4), :] = value[:, lanes]


def spread(planes, out_ref, rows):
    source, target = iota((2 * LANES, 4 * LANES), 0), iota((2 * LANES, 4 * LANES), 1)
    first = jnp.where(source < LANES, 4 * source, 4 * (source - LANES) + 1)
    places = [one_hot(target == first + 2 * pair) for pair in range(2)]
    for part in range(planes.shape[0] // 4):
        value = None
        for pair, place in enumerate(places):
            at = 4 * part + 2 * pair
            plane = jnp.concatenate([planes[at, rows], planes[at + 1, rows]], axis=1)
            high = plane.astype(BF16)
            low = (plane - high.astype(F32)).astype(BF16)
            term = jnp.dot(high, place, preferred_element_type=F32)
            term = term + jnp.dot(low, place, preferred_element_type=F32)
            value = term if value is None else value + term
        out_ref[rows, part * 4 * LANES : (part + 1) * 4 * LANES] = value


def edge_kernel(starts, lengths, slot, *rest):
    up, down = rest[-2:]
    waves, block, _ = starts.shape
    for out, rows in ((up, slice(0, MARGIN)), (down, slice(block - MARGIN, block))):
        out[:waves] = starts[:, rows]
        out[waves : 2 * waves] = lengths[:, rows]
        out[2 * waves] = slot[rows]


def edge_traces(starts, lengths, slot, later):
    waves, _, columns = starts.shape
    shape = jax.ShapeDtypeStruct((2 * waves + 1, MARGIN, columns), jnp.int32)
    return pl.pallas_call(
        edge_kernel,
        in_specs=[pl.BlockSpec(memory_space=pltpu.VMEM)] * 3
        + [pl.BlockSpec(memory_space=pl.ANY)] * len(later),
        out_specs=[pl.BlockSpec(memory_space=pltpu.VMEM)] * 2,
        out_shape=[shape] * 2,
        compiler_params=pltpu.CompilerParams(vmem_limit_bytes=VMEM_LIMIT),
        cost_estimate=pl.CostEstimate(flops=1, bytes_accessed=1, transcendentals=0),
        name="edge_traces",
    )(starts, lengths, slot, *later)


def tile_kernel(waves, place_ref, *rest):
    tiles, rest = rest[:waves], rest[waves:]
    starts, lengths, slot, above, below, out_ref, amounts, masks, slots, planes = rest
    block, columns = slot.shape
    lens0 = place_ref[0] * block
    own = slice(MARGIN, block + MARGIN)
    edges = ((slice(0, MARGIN), above), (slice(block + MARGIN, block + 2 * MARGIN), below))
    slots[own] = slot[...]
    for rows, edge in edges:
        slots[rows] = edge[2 * waves]
    for hop in range(waves):
        which = place_ref[1] ^ hop
        tile = tiles[hop][...].astype(F32)
        parts = [(own, starts[which], lengths[which])]
        parts += [(rows, edge[which], edge[waves + which]) for rows, edge in edges]
        for rows, start, length in parts:
            lens = lens0 + rows.start - MARGIN + iota(start.shape, 0)
            amounts[which, rows] = tile[rows] / jnp.maximum(length, 1).astype(F32)
            masks[which, rows] = ((1 << length) - 1) << jnp.maximum(start - 4 * lens + OFFSET, 0)

    def body(group, _):
        at = pl.multiple_of(group * 8, 8)
        light = block_light(amounts, masks, slots, at, waves, shifts(waves))
        put_planes(light, planes, at * 4)
        return 0

    lax.fori_loop(0, block // 8, body, 0)
    spread(planes, out_ref, slice(0, 4 * block))


def tile_light(waves, place, tiles, starts, lengths, slot, above, below):
    block, columns = slot.shape
    high = block + 2 * MARGIN
    return pl.pallas_call(
        functools.partial(tile_kernel, waves),
        in_specs=[pl.BlockSpec(memory_space=pltpu.SMEM)]
        + [pl.BlockSpec(memory_space=pltpu.VMEM)] * (len(tiles) + 5),
        out_specs=pl.BlockSpec(memory_space=pltpu.VMEM),
        out_shape=jax.ShapeDtypeStruct((4 * block, 4 * columns), F32),
        scratch_shapes=[
            pltpu.VMEM((waves, high, columns), F32),
            pltpu.VMEM((waves, high, columns), jnp.int32),
            pltpu.VMEM((high, columns), jnp.int32),
            pltpu.VMEM((4 * columns // LANES, 4 * block, LANES), F32),
        ],
        compiler_params=pltpu.CompilerParams(vmem_limit_bytes=VMEM_LIMIT),
        cost_estimate=pl.CostEstimate(flops=1, bytes_accessed=1, transcendentals=0),
        name="tile_light",
    )(place, *tiles, starts, lengths, slot, above, below)


def exchange(pieces, axis):
    count = lax.axis_size(axis)
    received = list(pieces)
    for hop in sorted(range(1, count), key=lambda hop: ORDER.index(hop) if hop in ORDER else hop):
        pairs = [(source, source ^ hop) for source in range(count)]
        received[hop] = lax.ppermute(pieces[hop], axis, pairs)
    return received


def shifted(value, axis, steps):
    count = lax.axis_size(axis)
    initial, last = (max(0, -steps), min(count, count - steps))
    return lax.ppermute(value, axis, [(source, source + steps) for source in range(initial, last)])


def per_device(lyot_field, wave_scale, trace_start, trace_length, column_slot):
    parts, waves = lax.axis_size("row"), lax.axis_size("wave")
    block = column_slot.shape[0]
    row_index = lax.axis_index("row").astype(jnp.int32)
    wave_index = lax.axis_index("wave").astype(jnp.int32)
    me, wave = row_index.reshape(1), wave_index.reshape(1)
    place = jnp.stack([row_index, wave_index])
    halo = 4 * -(-max(shifts(waves)[1], -shifts(waves)[0]) // 4)
    layout = chunk_rows(block, halo)
    sent = []
    for ranges in layout:
        later = [sent[-1][hop] for hop in FIRST if hop < parts] if sent else []
        pieces = half_transform(ranges, parts, block, me, wave_scale, lyot_field[0], later)
        sent.append(exchange(pieces, "row"))
    later = [sent[NEAR[0]][hop] for hop in NEAR[1] if hop < parts]
    up, down = edge_traces(trace_start, trace_length, column_slot, later)
    above = shifted(down, "row", 1)
    below = shifted(up, "row", -1)
    later = [sent[-1][hop] for hop in AHEAD if hop < parts]
    table = lens_table(wave_scale, lyot_field.shape[3], [*later, above, below])
    intensity = lens_intensity(layout, parts, waves, block, me, wave, table, sent)
    tiles = exchange(intensity, "wave")
    return tile_light(
        waves, place, tiles, trace_start, trace_length, column_slot, above, below
    )


MARGIN = 8
ROOM = 48
AHEAD = (1, 2)
NEAR = (0, (1,))
ORDER = ()
WIDTH = 4096
SIZE = 512
FIRST = (0, 1, 2)


def solution(mesh):
    placed = (
        P("wave", "row", None, None),
        P("wave"),
        P(None, "row", "wave"),
        P(None, "row", "wave"),
        P("row", "wave"),
    )
    return jax.shard_map(
        per_device, mesh=mesh, in_specs=placed, out_specs=P("row", "wave"), check_vma=False
    )
```

```python
import functools
import math

import jax
import jax.numpy as jnp
from jax import lax
from jax.experimental import pallas as pl
from jax.experimental.pallas import tpu as pltpu
from jax.sharding import PartitionSpec as P

NQ = 1024
OFFSET = 8
LMAX = 8
LANES = 128
F32 = jnp.float32
BF16 = jnp.bfloat16
MIB = 1024 * 1024
VMEM_LIMIT = 20 * MIB


def iota(shape, dim):
    return lax.broadcasted_iota(jnp.int32, shape, dim)


def dot_nt(a, b):
    return lax.dot_general(a, b, (((1,), (1,)), ((), ())), preferred_element_type=F32)


def one_hot(mask):
    return jnp.where(mask, 1.0, 0.0).astype(BF16)


def cos_sin_turns(turns):
    angle = (turns - jnp.round(turns)) * math.pi
    square = angle * angle
    sine = jnp.full_like(angle, 1.0 / math.factorial(13))
    for order in (11, 9, 7, 5, 3, 1):
        sine = sine * square + (-1.0) ** ((order - 1) // 2) / math.factorial(order)
    sine = sine * angle
    cosine = jnp.full_like(angle, 1.0 / math.factorial(16))
    for order in (14, 12, 10, 8, 6, 4, 2, 0):
        cosine = cosine * square + (-1.0) ** (order // 2) / math.factorial(order)
    return 1.0 - 2.0 * sine * sine, 2.0 * sine * cosine


def chunk_rows(block, halo):
    edge = block // 4 - halo
    return (((-halo, edge), (block - edge, block + halo)), ((edge, block - edge),))


def count_of(ranges):
    return sum(stop - start for start, stop in ranges)


def start_turns(first, here, pupil, scale, turn, step):
    coarse = jnp.floor(scale * 4096.0) * (1.0 / 4096.0)
    fine = scale - coarse
    shape = (here.stop - here.start, LANES)
    lens = (iota(shape, 0) + first).astype(F32) - (NQ - 1) / 2.0
    place = iota(shape, 1).astype(F32) - (pupil - 1) / 2.0
    cosine, sine = cos_sin_turns(lens * place * (scale * (1.0 / pupil)))
    norm = 1.0 / math.sqrt(pupil)
    turn[0, here] = cosine * norm
    turn[1, here] = sine * norm
    whole = lens * coarse * (LANES / pupil)
    whole = whole - jnp.round(whole)
    cosine, sine = cos_sin_turns(whole + lens * fine * (LANES / pupil))
    step[0, here] = cosine
    step[1, here] = sine


def turn_table(low, high, turn, step, table):
    half = table.shape[0] // 2

    for start in range(low, high, LANES):
        cosine, sine = turn[0], turn[1]
        table[:half, start : start + LANES] = cosine.astype(BF16)
        table[half:, start : start + LANES] = sine.astype(BF16)
        turn[0] = cosine * step[0] - sine * step[1]
        turn[1] = sine * step[0] + cosine * step[1]


def table_kernel(scale_ref, *rest):
    table, turn, step = rest[-3:]
    half, pupil = table.shape[0] // 2, table.shape[1]
    for low in range(0, half, 64):
        here = slice(low, min(low + 64, half))
        start_turns(low, here, pupil, scale_ref[0], turn, step)
        rotation = step[0, here], step[1, here]
        cosine, sine = turn[0, here], turn[1, here]
        for start in range(0, pupil, LANES):
            table[here, start : start + LANES] = cosine.astype(BF16)
            table[half + low : half + here.stop, start : start + LANES] = sine.astype(BF16)
            cosine, sine = (
                cosine * rotation[0] - sine * rotation[1],
                sine * rotation[0] + cosine * rotation[1],
            )


def lens_table(scale, pupil, later):
    return pl.pallas_call(
        table_kernel,
        in_specs=[pl.BlockSpec(memory_space=pltpu.SMEM)]
        + [pl.BlockSpec(memory_space=pl.ANY)] * len(later),
        out_specs=pl.BlockSpec(memory_space=pltpu.VMEM),
        out_shape=jax.ShapeDtypeStruct((NQ, pupil), BF16),
        scratch_shapes=[pltpu.VMEM((2, NQ // 2, LANES), F32)] * 2,
        compiler_params=pltpu.CompilerParams(vmem_limit_bytes=VMEM_LIMIT),
        cost_estimate=pl.CostEstimate(flops=1, bytes_accessed=1, transcendentals=0),
        name="lens_table",
    )(scale, *later)


def half_kernel(ranges, parts, block, width, size, extra, me_ref, scale_ref, field_hbm, *rest):
    outs = rest[extra : extra + parts]
    field, table, turn, step, halves, arrived = rest[extra + parts :]
    samples, _, pupil = field_hbm.shape
    half = table.shape[0] // 2
    rows = count_of(ranges)
    loads = {}
    for piece in range(samples // size):
        for low in range(0, pupil, width):
            here = (pl.ds(piece * size, size), slice(None), pl.ds(low, width))
            loads[piece, low] = pltpu.make_async_copy(
                field_hbm.at[here], field.at[here], arrived.at[len(loads)]
            )
            loads[piece, low].start()

    at = 0
    for group in range(parts // 2):
        for low, high in ranges:
            here = slice(at, at + high - low)
            start_turns(group * block + low, here, pupil, scale_ref[0], turn, step)
            at += high - low
    source, target = iota((2 * LANES, 2 * LANES), 0), iota((2 * LANES, 2 * LANES), 1)
    apart = one_hot(source == jnp.where(target < LANES, 2 * target, 2 * (target - LANES) + 1))
    for piece in range(samples // size):
        product = None
        for low in range(0, pupil, width):
            lanes = slice(low, low + width)
            if piece == 0:
                turn_table(low, low + width, turn, step, table)
            loads[piece, low].wait()
            here = field[piece * size : (piece + 1) * size, :, lanes].reshape(2 * size, width)
            term = dot_nt(table[:, lanes], here)
            product = term if product is None else product + term
        for inner in range(size // LANES):
            even_odd = []
            for side in range(2):
                lanes = slice((2 * inner + side) * LANES, (2 * inner + side + 1) * LANES)
                direct, cross = product[:half, lanes], product[half:, lanes]
                swapped = jnp.where(
                    iota(cross.shape, 1) % 2 == 0,
                    pltpu.roll(cross, LANES - 1, 1),
                    -pltpu.roll(cross, 1, 1),
                )
                even_odd.append((direct + swapped, direct - swapped))
            first = piece * size + inner * LANES
            lanes = slice(first, first + LANES)
            for mirrored in range(2):
                both = jnp.concatenate([pair[mirrored] for pair in even_odd], axis=1)
                both = jnp.dot(both.astype(BF16), apart, preferred_element_type=F32)
                for group in range(parts // 2):
                    owner = parts - 1 - group if mirrored else group
                    here = slice(group * rows, (group + 1) * rows)
                    halves[owner, :rows, lanes] = both[here, :LANES].astype(BF16)
                    halves[owner, rows:, lanes] = both[here, LANES:].astype(BF16)
    for hop in range(parts):
        outs[hop][...] = halves[me_ref[0] ^ hop]


def half_transform(ranges, parts, block, me, scale, field, later):
    samples, _, pupil = field.shape
    rows = count_of(ranges)
    height = parts * rows
    width, size = min(WIDTH, pupil), min(SIZE, samples)
    return pl.pallas_call(
        functools.partial(half_kernel, ranges, parts, block, width, size, len(later)),
        in_specs=[pl.BlockSpec(memory_space=pltpu.SMEM)] * 2
        + [pl.BlockSpec(memory_space=pl.ANY)] * (1 + len(later)),
        out_specs=[pl.BlockSpec(memory_space=pltpu.VMEM)] * parts,
        scratch_shapes=[
            pltpu.VMEM(field.shape, BF16),
            pltpu.VMEM((height, pupil), BF16),
            pltpu.VMEM((2, height // 2, LANES), F32),
            pltpu.VMEM((2, height // 2, LANES), F32),
            pltpu.VMEM((parts, 2 * rows, samples), BF16),
            pltpu.SemaphoreType.DMA((pupil // width * (samples // size),)),
        ],
        out_shape=[jax.ShapeDtypeStruct((2 * rows, samples), BF16)] * parts,
        compiler_params=pltpu.CompilerParams(vmem_limit_bytes=ROOM * MIB),
        cost_estimate=pl.CostEstimate(flops=1, bytes_accessed=1, transcendentals=0),
        name="half_transform",
    )(me, scale, field, *later)


def lens_kernel(layout, parts, waves, block, extra, me_ref, wave_ref, table, *rest):
    kinds = len(layout)
    pieces, rest = rest[: kinds * parts], rest[kinds * parts :]
    outs, tiles = rest[extra : extra + waves], rest[extra + waves]
    me, wave = me_ref[0], wave_ref[0]
    half = table.shape[0] // 2
    samples = pieces[0].shape[1]
    total = None
    for hop in range(parts):
        near = [pieces[kind * parts + hop][...] for kind in range(kinds)]
        lanes = pl.ds(pl.multiple_of((me ^ hop) * samples, samples), samples)
        term = dot_nt(jnp.concatenate(near, axis=0), table[:, lanes])
        total = term if hop == 0 else total + term

    strips, spans, at = ([], []), [], 0
    for ranges in layout:
        rows = count_of(ranges)
        real, imag = total[at : at + rows], total[at + rows : at + 2 * rows]
        at += 2 * rows
        for mirrored, sign in enumerate((1.0, -1.0)):
            lens_real = real[:, :half] + sign * imag[:, half:]
            lens_imag = imag[:, :half] - sign * real[:, half:]
            strips[mirrored].append(lens_real * lens_real + lens_imag * lens_imag)
        spans.extend(ranges)
    height, columns = tiles.shape[1:]
    count = sum(count_of(ranges) for ranges in layout)
    held = iota((height, count), 1)
    row, at = jnp.zeros((height, count), jnp.int32), 0
    for low, high in spans:
        row = jnp.where(held >= at, held - at + low, row)
        at += high - low
    row = jnp.where(me >= parts // 2, block - 1 - row, row)
    pick = one_hot(row == iota((height, count), 0) - MARGIN)
    back = one_hot(iota((columns, columns), 0) == columns - 1 - iota((columns, columns), 1))
    for mirrored in range(2):
        strip = jnp.concatenate(strips[mirrored], axis=0).astype(BF16)
        strip = jnp.dot(pick, strip, preferred_element_type=F32).astype(BF16)
        for group in range(waves // 2):
            tile = strip[:, group * columns : (group + 1) * columns]
            if mirrored:
                tile = jnp.dot(tile, back, preferred_element_type=F32).astype(BF16)
            tiles[waves - 1 - group if mirrored else group] = tile
    for hop in range(waves):
        outs[hop][...] = tiles[wave ^ hop]


def lens_intensity(layout, parts, waves, block, me, wave, table, sent, later):
    shape = (block + 2 * MARGIN, NQ // waves)
    pieces = [piece for part in sent for piece in part]
    return pl.pallas_call(
        functools.partial(lens_kernel, layout, parts, waves, block, len(later)),
        in_specs=[pl.BlockSpec(memory_space=pltpu.SMEM)] * 2
        + [pl.BlockSpec(memory_space=pltpu.VMEM)] * (1 + len(pieces))
        + [pl.BlockSpec(memory_space=pl.ANY)] * len(later),
        out_specs=[pl.BlockSpec(memory_space=pltpu.VMEM)] * waves,
        out_shape=[jax.ShapeDtypeStruct(shape, BF16)] * waves,
        scratch_shapes=[pltpu.VMEM((waves, *shape), BF16)],
        compiler_params=pltpu.CompilerParams(vmem_limit_bytes=VMEM_LIMIT),
        cost_estimate=pl.CostEstimate(flops=1, bytes_accessed=1, transcendentals=0),
        name="lens_intensity",
    )(me, wave, table, *pieces, *later)


def shifts(waves):
    return -(OFFSET // 4), (waves - 1 + OFFSET - 1 + LMAX - 1) // 4


def block_light(amounts, masks, slots, at, lanes, waves, reach):
    light = [[None] * 4 for _ in range(4)]
    near = pl.ds(at, 24)
    slots_near = slots[near, lanes]
    values_near = [amounts[wave, near, lanes] for wave in range(waves)]
    masks_near = [masks[wave, near, lanes] for wave in range(waves)]
    for shift in range(reach[0], reach[1] + 1):
        rows = slice(8 - shift, 16 - shift)
        slot = slots_near[rows]
        value = [held[rows] for held in values_near]
        mask = [held[rows] for held in masks_near]
        picks = [slot == which for which in range(4)]
        for step in range(4):
            height = 4 * shift + step
            strip = None
            for wave in range(waves):
                if not wave - OFFSET <= height <= wave + OFFSET + LMAX - 2:
                    continue
                bit = (mask[wave] & (1 << (height + OFFSET))) != 0
                term = jnp.where(bit, value[wave], 0.0)
                strip = term if strip is None else strip + term
            if strip is None:
                continue
            for which in range(4):
                term = jnp.where(picks[which], strip, 0.0)
                held = light[step][which]
                light[step][which] = term if held is None else held + term
    return light


def put_planes(light, planes, at, part):
    for step in range(4):
        for which in range(4):
            planes.at[4 * part + which][pl.Slice(at + step, 8, 4), :] = light[step][which]


def spread(planes, out_ref, rows):
    source, target = iota((2 * LANES, 4 * LANES), 0), iota((2 * LANES, 4 * LANES), 1)
    first = jnp.where(source < LANES, 4 * source, 4 * (source - LANES) + 1)
    places = [one_hot(target == first + 2 * pair) for pair in range(2)]
    for part in range(planes.shape[0] // 4):
        value = None
        for pair, place in enumerate(places):
            at = 4 * part + 2 * pair
            plane = jnp.concatenate([planes[at, rows], planes[at + 1, rows]], axis=1)
            high = plane.astype(BF16)
            low = (plane - high.astype(F32)).astype(BF16)
            term = jnp.dot(high, place, preferred_element_type=F32)
            term = term + jnp.dot(low, place, preferred_element_type=F32)
            value = term if value is None else value + term
        out_ref[rows, part * 4 * LANES : (part + 1) * 4 * LANES] = value


def edge_kernel(starts, lengths, slot, *rest):
    up, down = rest[-2:]
    waves, block, _ = starts.shape
    for out, rows in ((up, slice(0, MARGIN)), (down, slice(block - MARGIN, block))):
        out[:waves] = starts[:, rows]
        out[waves : 2 * waves] = lengths[:, rows]
        out[2 * waves] = slot[rows]


def edge_traces(starts, lengths, slot, later):
    waves, _, columns = starts.shape
    shape = jax.ShapeDtypeStruct((2 * waves + 1, MARGIN, columns), jnp.int32)
    return pl.pallas_call(
        edge_kernel,
        in_specs=[pl.BlockSpec(memory_space=pltpu.VMEM)] * 3
        + [pl.BlockSpec(memory_space=pl.ANY)] * len(later),
        out_specs=[pl.BlockSpec(memory_space=pltpu.VMEM)] * 2,
        out_shape=[shape] * 2,
        compiler_params=pltpu.CompilerParams(vmem_limit_bytes=VMEM_LIMIT),
        cost_estimate=pl.CostEstimate(flops=1, bytes_accessed=1, transcendentals=0),
        name="edge_traces",
    )(starts, lengths, slot, *later)


def tile_kernel(waves, place_ref, *rest):
    tiles, rest = rest[:waves], rest[waves:]
    starts, lengths, slot, above, below, out_ref, amounts, masks, slots, planes = rest
    block, columns = slot.shape
    lens0 = place_ref[0] * block
    own = slice(MARGIN, block + MARGIN)
    edges = ((slice(0, MARGIN), above), (slice(block + MARGIN, block + 2 * MARGIN), below))
    slots[own] = slot[...]
    for rows, edge in edges:
        slots[rows] = edge[2 * waves]
    for hop in range(waves):
        which = place_ref[1] ^ hop
        tile = tiles[hop][...].astype(F32)
        parts = [(own, starts[which], lengths[which])]
        parts += [(rows, edge[which], edge[waves + which]) for rows, edge in edges]
        for rows, start, length in parts:
            lens = lens0 + rows.start - MARGIN + iota(start.shape, 0)
            amounts[which, rows] = tile[rows] / jnp.maximum(length, 1).astype(F32)
            masks[which, rows] = ((1 << length) - 1) << jnp.maximum(start - 4 * lens + OFFSET, 0)

    def body(group, _):
        at = pl.multiple_of(group * 8, 8)
        for part in range(columns // LANES):
            lanes = slice(part * LANES, (part + 1) * LANES)
            light = block_light(amounts, masks, slots, at, lanes, waves, shifts(waves))
            put_planes(light, planes, at * 4, part)
        return 0

    lax.fori_loop(0, block // 8, body, 0)
    spread(planes, out_ref, slice(0, 4 * block))


def tile_light(waves, place, tiles, starts, lengths, slot, above, below):
    block, columns = slot.shape
    high = block + 2 * MARGIN
    return pl.pallas_call(
        functools.partial(tile_kernel, waves),
        in_specs=[pl.BlockSpec(memory_space=pltpu.SMEM)]
        + [pl.BlockSpec(memory_space=pltpu.VMEM)] * (len(tiles) + 5),
        out_specs=pl.BlockSpec(memory_space=pltpu.VMEM),
        out_shape=jax.ShapeDtypeStruct((4 * block, 4 * columns), F32),
        scratch_shapes=[
            pltpu.VMEM((waves, high, columns), F32),
            pltpu.VMEM((waves, high, columns), jnp.int32),
            pltpu.VMEM((high, columns), jnp.int32),
            pltpu.VMEM((4 * columns // LANES, 4 * block, LANES), F32),
        ],
        compiler_params=pltpu.CompilerParams(vmem_limit_bytes=VMEM_LIMIT),
        cost_estimate=pl.CostEstimate(flops=1, bytes_accessed=1, transcendentals=0),
        name="tile_light",
    )(place, *tiles, starts, lengths, slot, above, below)


def exchange(pieces, axis):
    count = lax.axis_size(axis)
    received = list(pieces)
    for hop in sorted(range(1, count), key=lambda hop: ORDER.index(hop) if hop in ORDER else hop):
        pairs = [(source, source ^ hop) for source in range(count)]
        received[hop] = lax.ppermute(pieces[hop], axis, pairs)
    return received


def shifted(value, axis, steps):
    count = lax.axis_size(axis)
    initial, last = (max(0, -steps), min(count, count - steps))
    return lax.ppermute(value, axis, [(source, source + steps) for source in range(initial, last)])


def per_device(lyot_field, wave_scale, trace_start, trace_length, column_slot):
    parts, waves = lax.axis_size("row"), lax.axis_size("wave")
    block = column_slot.shape[0]
    row_index = lax.axis_index("row").astype(jnp.int32)
    wave_index = lax.axis_index("wave").astype(jnp.int32)
    me, wave = row_index.reshape(1), wave_index.reshape(1)
    place = jnp.stack([row_index, wave_index])
    halo = 4 * -(-max(shifts(waves)[1], -shifts(waves)[0]) // 4)
    layout = chunk_rows(block, halo)
    sent = []
    for ranges in layout:
        later = [sent[-1][hop] for hop in FIRST if hop < parts] if sent else []
        pieces = half_transform(ranges, parts, block, me, wave_scale, lyot_field[0], later)
        sent.append(exchange(pieces, "row"))
    later = [sent[-1][hop] for hop in AHEAD if hop < parts]
    up, down = edge_traces(trace_start, trace_length, column_slot, later)
    above = shifted(down, "row", 1)
    below = shifted(up, "row", -1)
    table = lens_table(wave_scale, lyot_field.shape[3], [*later, up])
    later = [above, below]
    intensity = lens_intensity(layout, parts, waves, block, me, wave, table, sent, later)
    tiles = exchange(intensity, "wave")
    return tile_light(
        waves, place, tiles, trace_start, trace_length, column_slot, above, below
    )


MARGIN = 8
ROOM = 48
AHEAD = (1, 2)
ORDER = ()
WIDTH = 4096
SIZE = 512
FIRST = (0, 1, 2)


def solution(mesh):
    placed = (
        P("wave", "row", None, None),
        P("wave"),
        P(None, "row", "wave"),
        P(None, "row", "wave"),
        P("row", "wave"),
    )
    return jax.shard_map(
        per_device, mesh=mesh, in_specs=placed, out_specs=P("row", "wave"), check_vma=False
    )
```

```python
import functools
import math

import jax
import jax.numpy as jnp
from jax import lax
from jax.experimental import pallas as pl
from jax.experimental.pallas import tpu as pltpu
from jax.sharding import PartitionSpec as P

NQ = 1024
OFFSET = 8
LMAX = 8
LANES = 128
F32 = jnp.float32
BF16 = jnp.bfloat16
MIB = 1024 * 1024
VMEM_LIMIT = 20 * MIB


def iota(shape, dim):
    return lax.broadcasted_iota(jnp.int32, shape, dim)


def dot_nt(a, b):
    return lax.dot_general(a, b, (((1,), (1,)), ((), ())), preferred_element_type=F32)


def one_hot(mask):
    return jnp.where(mask, 1.0, 0.0).astype(BF16)


def cos_sin_turns(turns):
    angle = (turns - jnp.round(turns)) * math.pi
    square = angle * angle
    sine = jnp.full_like(angle, 1.0 / math.factorial(13))
    for order in (11, 9, 7, 5, 3, 1):
        sine = sine * square + (-1.0) ** ((order - 1) // 2) / math.factorial(order)
    sine = sine * angle
    cosine = jnp.full_like(angle, 1.0 / math.factorial(16))
    for order in (14, 12, 10, 8, 6, 4, 2, 0):
        cosine = cosine * square + (-1.0) ** (order // 2) / math.factorial(order)
    return 1.0 - 2.0 * sine * sine, 2.0 * sine * cosine


def count_of(ranges):
    return sum(stop - start for start, stop in ranges)


def start_turns(first, here, pupil, scale, turn, step):
    coarse = jnp.floor(scale * 4096.0) * (1.0 / 4096.0)
    fine = scale - coarse
    shape = (here.stop - here.start, LANES)
    lens = (iota(shape, 0) + first).astype(F32) - (NQ - 1) / 2.0
    place = iota(shape, 1).astype(F32) - (pupil - 1) / 2.0
    cosine, sine = cos_sin_turns(lens * place * (scale * (1.0 / pupil)))
    norm = 1.0 / math.sqrt(pupil)
    turn[0, here] = cosine * norm
    turn[1, here] = sine * norm
    whole = lens * coarse * (LANES / pupil)
    whole = whole - jnp.round(whole)
    cosine, sine = cos_sin_turns(whole + lens * fine * (LANES / pupil))
    step[0, here] = cosine
    step[1, here] = sine


def turn_table(low, high, turn, step, table):
    half = table.shape[0] // 2

    for start in range(low, high, LANES):
        cosine, sine = turn[0], turn[1]
        table[:half, start : start + LANES] = cosine.astype(BF16)
        table[half:, start : start + LANES] = sine.astype(BF16)
        turn[0] = cosine * step[0] - sine * step[1]
        turn[1] = sine * step[0] + cosine * step[1]


def table_kernel(scale_ref, *rest):
    table, turn, step = rest[-3:]
    half, pupil = table.shape[0] // 2, table.shape[1]
    for low in range(0, half, 64):
        here = slice(low, min(low + 64, half))
        start_turns(low, here, pupil, scale_ref[0], turn, step)
        rotation = step[0, here], step[1, here]
        cosine, sine = turn[0, here], turn[1, here]
        for start in range(0, pupil, LANES):
            table[here, start : start + LANES] = cosine.astype(BF16)
            table[half + low : half + here.stop, start : start + LANES] = sine.astype(BF16)
            cosine, sine = (
                cosine * rotation[0] - sine * rotation[1],
                sine * rotation[0] + cosine * rotation[1],
            )


def lens_table(scale, pupil, later):
    return pl.pallas_call(
        table_kernel,
        in_specs=[pl.BlockSpec(memory_space=pltpu.SMEM)]
        + [pl.BlockSpec(memory_space=pl.ANY)] * len(later),
        out_specs=pl.BlockSpec(memory_space=pltpu.VMEM),
        out_shape=jax.ShapeDtypeStruct((NQ, pupil), BF16),
        scratch_shapes=[pltpu.VMEM((2, NQ // 2, LANES), F32)] * 2,
        compiler_params=pltpu.CompilerParams(vmem_limit_bytes=VMEM_LIMIT),
        cost_estimate=pl.CostEstimate(flops=1, bytes_accessed=1, transcendentals=0),
        name="lens_table",
    )(scale, *later)


def half_kernel(ranges, parts, block, width, size, extra, me_ref, scale_ref, field_hbm, *rest):
    outs = rest[extra : extra + parts]
    field, table, turn, step, halves, arrived = rest[extra + parts :]
    samples, _, pupil = field_hbm.shape
    half = table.shape[0] // 2
    rows = count_of(ranges)
    loads = {}
    for piece in range(samples // size):
        for low in range(0, pupil, width):
            here = (pl.ds(piece * size, size), slice(None), pl.ds(low, width))
            loads[piece, low] = pltpu.make_async_copy(
                field_hbm.at[here], field.at[here], arrived.at[len(loads)]
            )
            loads[piece, low].start()

    at = 0
    for group in range(parts // 2):
        for low, high in ranges:
            here = slice(at, at + high - low)
            start_turns(group * block + low, here, pupil, scale_ref[0], turn, step)
            at += high - low
    source, target = iota((2 * LANES, 2 * LANES), 0), iota((2 * LANES, 2 * LANES), 1)
    apart = one_hot(source == jnp.where(target < LANES, 2 * target, 2 * (target - LANES) + 1))
    for piece in range(samples // size):
        product = None
        for low in range(0, pupil, width):
            lanes = slice(low, low + width)
            if piece == 0:
                turn_table(low, low + width, turn, step, table)
            loads[piece, low].wait()
            here = field[piece * size : (piece + 1) * size, :, lanes].reshape(2 * size, width)
            term = dot_nt(table[:, lanes], here)
            product = term if product is None else product + term
        for inner in range(size // LANES):
            even_odd = []
            for side in range(2):
                lanes = slice((2 * inner + side) * LANES, (2 * inner + side + 1) * LANES)
                direct, cross = product[:half, lanes], product[half:, lanes]
                swapped = jnp.where(
                    iota(cross.shape, 1) % 2 == 0,
                    pltpu.roll(cross, LANES - 1, 1),
                    -pltpu.roll(cross, 1, 1),
                )
                even_odd.append((direct + swapped, direct - swapped))
            first = piece * size + inner * LANES
            lanes = slice(first, first + LANES)
            for mirrored in range(2):
                both = jnp.concatenate([pair[mirrored] for pair in even_odd], axis=1)
                both = jnp.dot(both.astype(BF16), apart, preferred_element_type=F32)
                for group in range(parts // 2):
                    owner = parts - 1 - group if mirrored else group
                    here = slice(group * rows, (group + 1) * rows)
                    halves[owner, :rows, lanes] = both[here, :LANES].astype(BF16)
                    halves[owner, rows:, lanes] = both[here, LANES:].astype(BF16)
    for hop in range(parts):
        outs[hop][...] = halves[me_ref[0] ^ hop]


def half_transform(ranges, parts, block, me, scale, field, later):
    samples, _, pupil = field.shape
    rows = count_of(ranges)
    height = parts * rows
    width, size = min(WIDTH, pupil), min(SIZE, samples)
    return pl.pallas_call(
        functools.partial(half_kernel, ranges, parts, block, width, size, len(later)),
        in_specs=[pl.BlockSpec(memory_space=pltpu.SMEM)] * 2
        + [pl.BlockSpec(memory_space=pl.ANY)] * (1 + len(later)),
        out_specs=[pl.BlockSpec(memory_space=pltpu.VMEM)] * parts,
        scratch_shapes=[
            pltpu.VMEM(field.shape, BF16),
            pltpu.VMEM((height, pupil), BF16),
            pltpu.VMEM((2, height // 2, LANES), F32),
            pltpu.VMEM((2, height // 2, LANES), F32),
            pltpu.VMEM((parts, 2 * rows, samples), BF16),
            pltpu.SemaphoreType.DMA((pupil // width * (samples // size),)),
        ],
        out_shape=[jax.ShapeDtypeStruct((2 * rows, samples), BF16)] * parts,
        compiler_params=pltpu.CompilerParams(vmem_limit_bytes=ROOM * MIB),
        cost_estimate=pl.CostEstimate(flops=1, bytes_accessed=1, transcendentals=0),
        name="half_transform",
    )(me, scale, field, *later)


def lens_kernel(layout, parts, waves, block, extra, me_ref, wave_ref, table, *rest):
    kinds = len(layout)
    pieces, rest = rest[: kinds * parts], rest[kinds * parts :]
    outs, tiles = rest[extra : extra + waves], rest[extra + waves]
    me, wave = me_ref[0], wave_ref[0]
    half = table.shape[0] // 2
    samples = pieces[0].shape[1]
    total = None
    for hop in range(parts):
        near = [pieces[kind * parts + hop][...] for kind in range(kinds)]
        lanes = pl.ds(pl.multiple_of((me ^ hop) * samples, samples), samples)
        term = dot_nt(jnp.concatenate(near, axis=0), table[:, lanes])
        total = term if hop == 0 else total + term

    strips, spans, at = ([], []), [], 0
    for ranges in layout:
        rows = count_of(ranges)
        real, imag = total[at : at + rows], total[at + rows : at + 2 * rows]
        at += 2 * rows
        for mirrored, sign in enumerate((1.0, -1.0)):
            lens_real = real[:, :half] + sign * imag[:, half:]
            lens_imag = imag[:, :half] - sign * real[:, half:]
            strips[mirrored].append(lens_real * lens_real + lens_imag * lens_imag)
        spans.extend(ranges)
    height, columns = tiles.shape[1:]
    count = sum(count_of(ranges) for ranges in layout)
    held = iota((height, count), 1)
    row, at = jnp.zeros((height, count), jnp.int32), 0
    for low, high in spans:
        row = jnp.where(held >= at, held - at + low, row)
        at += high - low
    row = jnp.where(me >= parts // 2, block - 1 - row, row)
    pick = one_hot(row == iota((height, count), 0) - MARGIN)
    back = one_hot(iota((columns, columns), 0) == columns - 1 - iota((columns, columns), 1))
    for mirrored in range(2):
        strip = jnp.concatenate(strips[mirrored], axis=0).astype(BF16)
        strip = jnp.dot(pick, strip, preferred_element_type=F32).astype(BF16)
        for group in range(waves // 2):
            tile = strip[:, group * columns : (group + 1) * columns]
            if mirrored:
                tile = jnp.dot(tile, back, preferred_element_type=F32).astype(BF16)
            tiles[waves - 1 - group if mirrored else group] = tile
    for hop in range(waves):
        outs[hop][...] = tiles[wave ^ hop]


def lens_intensity(layout, parts, waves, block, me, wave, table, sent, later):
    shape = (block + 2 * MARGIN, NQ // waves)
    pieces = [piece for part in sent for piece in part]
    return pl.pallas_call(
        functools.partial(lens_kernel, layout, parts, waves, block, len(later)),
        in_specs=[pl.BlockSpec(memory_space=pltpu.SMEM)] * 2
        + [pl.BlockSpec(memory_space=pltpu.VMEM)] * (1 + len(pieces))
        + [pl.BlockSpec(memory_space=pl.ANY)] * len(later),
        out_specs=[pl.BlockSpec(memory_space=pltpu.VMEM)] * waves,
        out_shape=[jax.ShapeDtypeStruct(shape, BF16)] * waves,
        scratch_shapes=[pltpu.VMEM((waves, *shape), BF16)],
        compiler_params=pltpu.CompilerParams(vmem_limit_bytes=VMEM_LIMIT),
        cost_estimate=pl.CostEstimate(flops=1, bytes_accessed=1, transcendentals=0),
        name="lens_intensity",
    )(me, wave, table, *pieces, *later)


def shifts(waves):
    return -(OFFSET // 4), (waves - 1 + OFFSET - 1 + LMAX - 1) // 4


def block_light(amounts, masks, slots, at, lanes, waves, reach):
    light = [[None] * 4 for _ in range(4)]
    near = pl.ds(at, 24)
    slots_near = slots[near, lanes]
    values_near = [amounts[wave, near, lanes] for wave in range(waves)]
    masks_near = [masks[wave, near, lanes] for wave in range(waves)]
    for shift in range(reach[0], reach[1] + 1):
        rows = slice(8 - shift, 16 - shift)
        slot = slots_near[rows]
        value = [held[rows] for held in values_near]
        mask = [held[rows] for held in masks_near]
        picks = [slot == which for which in range(4)]
        for step in range(4):
            height = 4 * shift + step
            strip = None
            for wave in range(waves):
                if not wave - OFFSET <= height <= wave + OFFSET + LMAX - 2:
                    continue
                bit = (mask[wave] & (1 << (height + OFFSET))) != 0
                term = jnp.where(bit, value[wave], 0.0)
                strip = term if strip is None else strip + term
            if strip is None:
                continue
            for which in range(4):
                term = jnp.where(picks[which], strip, 0.0)
                held = light[step][which]
                light[step][which] = term if held is None else held + term
    return light


def put_planes(light, planes, at, part):
    for step in range(4):
        for which in range(4):
            planes.at[4 * part + which][pl.Slice(at + step, 8, 4), :] = light[step][which]


def spread(planes, out_ref, rows):
    source, target = iota((2 * LANES, 4 * LANES), 0), iota((2 * LANES, 4 * LANES), 1)
    first = jnp.where(source < LANES, 4 * source, 4 * (source - LANES) + 1)
    places = [one_hot(target == first + 2 * pair) for pair in range(2)]
    for part in range(planes.shape[0] // 4):
        value = None
        for pair, place in enumerate(places):
            at = 4 * part + 2 * pair
            plane = jnp.concatenate([planes[at, rows], planes[at + 1, rows]], axis=1)
            high = plane.astype(BF16)
            low = (plane - high.astype(F32)).astype(BF16)
            term = jnp.dot(high, place, preferred_element_type=F32)
            term = term + jnp.dot(low, place, preferred_element_type=F32)
            value = term if value is None else value + term
        out_ref[rows, part * 4 * LANES : (part + 1) * 4 * LANES] = value


def edge_kernel(starts, lengths, slot, *rest):
    up, down = rest[-2:]
    waves, block, _ = starts.shape
    for out, rows in ((up, slice(0, MARGIN)), (down, slice(block - MARGIN, block))):
        out[:waves] = starts[:, rows]
        out[waves : 2 * waves] = lengths[:, rows]
        out[2 * waves] = slot[rows]


def edge_traces(starts, lengths, slot, later):
    waves, _, columns = starts.shape
    shape = jax.ShapeDtypeStruct((2 * waves + 1, MARGIN, columns), jnp.int32)
    return pl.pallas_call(
        edge_kernel,
        in_specs=[pl.BlockSpec(memory_space=pltpu.VMEM)] * 3
        + [pl.BlockSpec(memory_space=pl.ANY)] * len(later),
        out_specs=[pl.BlockSpec(memory_space=pltpu.VMEM)] * 2,
        out_shape=[shape] * 2,
        compiler_params=pltpu.CompilerParams(vmem_limit_bytes=VMEM_LIMIT),
        cost_estimate=pl.CostEstimate(flops=1, bytes_accessed=1, transcendentals=0),
        name="edge_traces",
    )(starts, lengths, slot, *later)


def tile_kernel(waves, place_ref, *rest):
    tiles, rest = rest[:waves], rest[waves:]
    starts, lengths, slot, above, below, out_ref, amounts, masks, slots, planes = rest
    block, columns = slot.shape
    lens0 = place_ref[0] * block
    own = slice(MARGIN, block + MARGIN)
    edges = ((slice(0, MARGIN), above), (slice(block + MARGIN, block + 2 * MARGIN), below))
    slots[own] = slot[...]
    for rows, edge in edges:
        slots[rows] = edge[2 * waves]
    for hop in range(waves):
        which = place_ref[1] ^ hop
        tile = tiles[hop][...].astype(F32)
        parts = [(own, starts[which], lengths[which])]
        parts += [(rows, edge[which], edge[waves + which]) for rows, edge in edges]
        for rows, start, length in parts:
            lens = lens0 + rows.start - MARGIN + iota(start.shape, 0)
            amounts[which, rows] = tile[rows] / jnp.maximum(length, 1).astype(F32)
            masks[which, rows] = ((1 << length) - 1) << jnp.maximum(start - 4 * lens + OFFSET, 0)

    def body(group, _):
        at = pl.multiple_of(group * 8, 8)
        for part in range(columns // LANES):
            lanes = slice(part * LANES, (part + 1) * LANES)
            light = block_light(amounts, masks, slots, at, lanes, waves, shifts(waves))
            put_planes(light, planes, at * 4, part)
        return 0

    lax.fori_loop(0, block // 8, body, 0)
    spread(planes, out_ref, slice(0, 4 * block))


def tile_light(waves, place, tiles, starts, lengths, slot, above, below):
    block, columns = slot.shape
    high = block + 2 * MARGIN
    return pl.pallas_call(
        functools.partial(tile_kernel, waves),
        in_specs=[pl.BlockSpec(memory_space=pltpu.SMEM)]
        + [pl.BlockSpec(memory_space=pltpu.VMEM)] * (len(tiles) + 5),
        out_specs=pl.BlockSpec(memory_space=pltpu.VMEM),
        out_shape=jax.ShapeDtypeStruct((4 * block, 4 * columns), F32),
        scratch_shapes=[
            pltpu.VMEM((waves, high, columns), F32),
            pltpu.VMEM((waves, high, columns), jnp.int32),
            pltpu.VMEM((high, columns), jnp.int32),
            pltpu.VMEM((4 * columns // LANES, 4 * block, LANES), F32),
        ],
        compiler_params=pltpu.CompilerParams(vmem_limit_bytes=VMEM_LIMIT),
        cost_estimate=pl.CostEstimate(flops=1, bytes_accessed=1, transcendentals=0),
        name="tile_light",
    )(place, *tiles, starts, lengths, slot, above, below)


def exchange(pieces, axis):
    count = lax.axis_size(axis)
    received = list(pieces)
    for hop in sorted(range(1, count), key=lambda hop: ORDER.index(hop) if hop in ORDER else hop):
        pairs = [(source, source ^ hop) for source in range(count)]
        received[hop] = lax.ppermute(pieces[hop], axis, pairs)
    return received


def shifted(value, axis, steps):
    count = lax.axis_size(axis)
    initial, last = (max(0, -steps), min(count, count - steps))
    return lax.ppermute(value, axis, [(source, source + steps) for source in range(initial, last)])


def per_device(lyot_field, wave_scale, trace_start, trace_length, column_slot):
    parts, waves = lax.axis_size("row"), lax.axis_size("wave")
    block = column_slot.shape[0]
    row_index = lax.axis_index("row").astype(jnp.int32)
    wave_index = lax.axis_index("wave").astype(jnp.int32)
    me, wave = row_index.reshape(1), wave_index.reshape(1)
    place = jnp.stack([row_index, wave_index])
    halo = 4 * -(-max(shifts(waves)[1], -shifts(waves)[0]) // 4)
    layout = (((-halo, block + halo),),)
    sent = []
    for ranges in layout:
        later = [sent[-1][hop] for hop in FIRST if hop < parts] if sent else []
        pieces = half_transform(ranges, parts, block, me, wave_scale, lyot_field[0], later)
        sent.append(exchange(pieces, "row"))
    later = [sent[-1][hop] for hop in AHEAD if hop < parts]
    up, down = edge_traces(trace_start, trace_length, column_slot, later)
    above = shifted(down, "row", 1)
    below = shifted(up, "row", -1)
    table = lens_table(wave_scale, lyot_field.shape[3], [*later, up])
    later = [above, below]
    intensity = lens_intensity(layout, parts, waves, block, me, wave, table, sent, later)
    tiles = exchange(intensity, "wave")
    return tile_light(
        waves, place, tiles, trace_start, trace_length, column_slot, above, below
    )


MARGIN = 8
ROOM = 48
AHEAD = (1, 2)
ORDER = ()
WIDTH = 4096
SIZE = 512
FIRST = (0, 1, 2)


def solution(mesh):
    placed = (
        P("wave", "row", None, None),
        P("wave"),
        P(None, "row", "wave"),
        P(None, "row", "wave"),
        P("row", "wave"),
    )
    return jax.shard_map(
        per_device, mesh=mesh, in_specs=placed, out_specs=P("row", "wave"), check_vma=False
    )
```

```python
import functools
import math

import jax
import jax.numpy as jnp
from jax import lax
from jax.experimental import pallas as pl
from jax.experimental.pallas import tpu as pltpu
from jax.sharding import PartitionSpec as P

NQ = 1024
OFFSET = 8
LMAX = 8
LANES = 128
F32 = jnp.float32
BF16 = jnp.bfloat16
MIB = 1024 * 1024
VMEM_LIMIT = 20 * MIB


def iota(shape, dim):
    return lax.broadcasted_iota(jnp.int32, shape, dim)


def dot_nt(a, b):
    return lax.dot_general(a, b, (((1,), (1,)), ((), ())), preferred_element_type=F32)


def one_hot(mask):
    return jnp.where(mask, 1.0, 0.0).astype(BF16)


def cos_sin_turns(turns):
    angle = (turns - jnp.round(turns)) * math.pi
    square = angle * angle
    sine = jnp.full_like(angle, 1.0 / math.factorial(13))
    for order in (11, 9, 7, 5, 3, 1):
        sine = sine * square + (-1.0) ** ((order - 1) // 2) / math.factorial(order)
    sine = sine * angle
    cosine = jnp.full_like(angle, 1.0 / math.factorial(16))
    for order in (14, 12, 10, 8, 6, 4, 2, 0):
        cosine = cosine * square + (-1.0) ** (order // 2) / math.factorial(order)
    return 1.0 - 2.0 * sine * sine, 2.0 * sine * cosine


def count_of(ranges):
    return sum(stop - start for start, stop in ranges)


def start_turns(first, here, pupil, scale, turn, step):
    coarse = jnp.floor(scale * 4096.0) * (1.0 / 4096.0)
    fine = scale - coarse
    shape = (here.stop - here.start, LANES)
    lens = (iota(shape, 0) + first).astype(F32) - (NQ - 1) / 2.0
    place = iota(shape, 1).astype(F32) - (pupil - 1) / 2.0
    cosine, sine = cos_sin_turns(lens * place * (scale * (1.0 / pupil)))
    norm = 1.0 / math.sqrt(pupil)
    turn[0, here] = cosine * norm
    turn[1, here] = sine * norm
    whole = lens * coarse * (LANES / pupil)
    whole = whole - jnp.round(whole)
    cosine, sine = cos_sin_turns(whole + lens * fine * (LANES / pupil))
    step[0, here] = cosine
    step[1, here] = sine


def turn_table(low, high, turn, step, table):
    half = table.shape[0] // 2

    for start in range(low, high, LANES):
        cosine, sine = turn[0], turn[1]
        table[:half, start : start + LANES] = cosine.astype(BF16)
        table[half:, start : start + LANES] = sine.astype(BF16)
        turn[0] = cosine * step[0] - sine * step[1]
        turn[1] = sine * step[0] + cosine * step[1]


def table_kernel(scale_ref, *rest):
    table, turn, step = rest[-3:]
    half, pupil = table.shape[0] // 2, table.shape[1]
    for low in range(0, half, 64):
        here = slice(low, min(low + 64, half))
        start_turns(low, here, pupil, scale_ref[0], turn, step)
        rotation = step[0, here], step[1, here]
        cosine, sine = turn[0, here], turn[1, here]
        for start in range(0, pupil, LANES):
            table[here, start : start + LANES] = cosine.astype(BF16)
            table[half + low : half + here.stop, start : start + LANES] = sine.astype(BF16)
            cosine, sine = (
                cosine * rotation[0] - sine * rotation[1],
                sine * rotation[0] + cosine * rotation[1],
            )


def lens_table(scale, pupil, later):
    return pl.pallas_call(
        table_kernel,
        in_specs=[pl.BlockSpec(memory_space=pltpu.SMEM)]
        + [pl.BlockSpec(memory_space=pl.ANY)] * len(later),
        out_specs=pl.BlockSpec(memory_space=pltpu.VMEM),
        out_shape=jax.ShapeDtypeStruct((NQ, pupil), BF16),
        scratch_shapes=[pltpu.VMEM((2, NQ // 2, LANES), F32)] * 2,
        compiler_params=pltpu.CompilerParams(vmem_limit_bytes=VMEM_LIMIT),
        cost_estimate=pl.CostEstimate(flops=1, bytes_accessed=1, transcendentals=0),
        name="lens_table",
    )(scale, *later)


def half_kernel(ranges, parts, block, width, size, extra, me_ref, scale_ref, field_hbm, *rest):
    outs = rest[extra : extra + parts]
    field, table, turn, step, halves, arrived = rest[extra + parts :]
    samples, _, pupil = field_hbm.shape
    half = table.shape[0] // 2
    rows = count_of(ranges)
    loads = {}
    for piece in range(samples // size):
        for low in range(0, pupil, width):
            here = (pl.ds(piece * size, size), slice(None), pl.ds(low, width))
            loads[piece, low] = pltpu.make_async_copy(
                field_hbm.at[here], field.at[here], arrived.at[len(loads)]
            )
            loads[piece, low].start()

    at = 0
    for group in range(parts // 2):
        for low, high in ranges:
            here = slice(at, at + high - low)
            start_turns(group * block + low, here, pupil, scale_ref[0], turn, step)
            at += high - low
    source, target = iota((2 * LANES, 2 * LANES), 0), iota((2 * LANES, 2 * LANES), 1)
    apart = one_hot(source == jnp.where(target < LANES, 2 * target, 2 * (target - LANES) + 1))
    for piece in range(samples // size):
        product = None
        for low in range(0, pupil, width):
            lanes = slice(low, low + width)
            if piece == 0:
                turn_table(low, low + width, turn, step, table)
            loads[piece, low].wait()
            here = field[piece * size : (piece + 1) * size, :, lanes].reshape(2 * size, width)
            term = dot_nt(table[:, lanes], here)
            product = term if product is None else product + term
        for inner in range(size // LANES):
            even_odd = []
            for side in range(2):
                lanes = slice((2 * inner + side) * LANES, (2 * inner + side + 1) * LANES)
                direct, cross = product[:half, lanes], product[half:, lanes]
                swapped = jnp.where(
                    iota(cross.shape, 1) % 2 == 0,
                    pltpu.roll(cross, LANES - 1, 1),
                    -pltpu.roll(cross, 1, 1),
                )
                even_odd.append((direct + swapped, direct - swapped))
            first = piece * size + inner * LANES
            lanes = slice(first, first + LANES)
            for mirrored in range(2):
                both = jnp.concatenate([pair[mirrored] for pair in even_odd], axis=1)
                both = jnp.dot(both.astype(BF16), apart, preferred_element_type=F32)
                for group in range(parts // 2):
                    owner = parts - 1 - group if mirrored else group
                    here = slice(group * rows, (group + 1) * rows)
                    halves[owner, :rows, lanes] = both[here, :LANES].astype(BF16)
                    halves[owner, rows:, lanes] = both[here, LANES:].astype(BF16)
    for hop in range(parts):
        outs[hop][...] = halves[me_ref[0] ^ hop]


def half_transform(ranges, parts, block, me, scale, field, later):
    samples, _, pupil = field.shape
    rows = count_of(ranges)
    height = parts * rows
    width, size = min(WIDTH, pupil), min(SIZE, samples)
    return pl.pallas_call(
        functools.partial(half_kernel, ranges, parts, block, width, size, len(later)),
        in_specs=[pl.BlockSpec(memory_space=pltpu.SMEM)] * 2
        + [pl.BlockSpec(memory_space=pl.ANY)] * (1 + len(later)),
        out_specs=[pl.BlockSpec(memory_space=pltpu.VMEM)] * parts,
        scratch_shapes=[
            pltpu.VMEM(field.shape, BF16),
            pltpu.VMEM((height, pupil), BF16),
            pltpu.VMEM((2, height // 2, LANES), F32),
            pltpu.VMEM((2, height // 2, LANES), F32),
            pltpu.VMEM((parts, 2 * rows, samples), BF16),
            pltpu.SemaphoreType.DMA((pupil // width * (samples // size),)),
        ],
        out_shape=[jax.ShapeDtypeStruct((2 * rows, samples), BF16)] * parts,
        compiler_params=pltpu.CompilerParams(vmem_limit_bytes=ROOM * MIB),
        cost_estimate=pl.CostEstimate(flops=1, bytes_accessed=1, transcendentals=0),
        name="half_transform",
    )(me, scale, field, *later)


def lens_kernel(layout, parts, waves, block, extra, me_ref, wave_ref, table, *rest):
    kinds = len(layout)
    pieces, rest = rest[: kinds * parts], rest[kinds * parts :]
    outs, tiles = rest[extra : extra + waves], rest[extra + waves]
    me, wave = me_ref[0], wave_ref[0]
    half = table.shape[0] // 2
    samples = pieces[0].shape[1]
    total = None
    for hop in range(parts):
        near = [pieces[kind * parts + hop][...] for kind in range(kinds)]
        lanes = pl.ds(pl.multiple_of((me ^ hop) * samples, samples), samples)
        term = dot_nt(jnp.concatenate(near, axis=0), table[:, lanes])
        total = term if hop == 0 else total + term

    strips, spans, at = ([], []), [], 0
    for ranges in layout:
        rows = count_of(ranges)
        real, imag = total[at : at + rows], total[at + rows : at + 2 * rows]
        at += 2 * rows
        for mirrored, sign in enumerate((1.0, -1.0)):
            lens_real = real[:, :half] + sign * imag[:, half:]
            lens_imag = imag[:, :half] - sign * real[:, half:]
            strips[mirrored].append(lens_real * lens_real + lens_imag * lens_imag)
        spans.extend(ranges)
    height, columns = tiles.shape[1:]
    count = sum(count_of(ranges) for ranges in layout)
    held = iota((height, count), 1)
    row, at = jnp.zeros((height, count), jnp.int32), 0
    for low, high in spans:
        row = jnp.where(held >= at, held - at + low, row)
        at += high - low
    row = jnp.where(me >= parts // 2, block - 1 - row, row)
    pick = one_hot(row == iota((height, count), 0) - MARGIN)
    back = one_hot(iota((columns, columns), 0) == columns - 1 - iota((columns, columns), 1))
    for mirrored in range(2):
        strip = jnp.concatenate(strips[mirrored], axis=0).astype(BF16)
        strip = jnp.dot(pick, strip, preferred_element_type=F32).astype(BF16)
        for group in range(waves // 2):
            tile = strip[:, group * columns : (group + 1) * columns]
            if mirrored:
                tile = jnp.dot(tile, back, preferred_element_type=F32).astype(BF16)
            tiles[waves - 1 - group if mirrored else group] = tile
    for hop in range(waves):
        outs[hop][...] = tiles[wave ^ hop]


def lens_intensity(layout, parts, waves, block, me, wave, table, sent, later):
    shape = (block + 2 * MARGIN, NQ // waves)
    pieces = [piece for part in sent for piece in part]
    return pl.pallas_call(
        functools.partial(lens_kernel, layout, parts, waves, block, len(later)),
        in_specs=[pl.BlockSpec(memory_space=pltpu.SMEM)] * 2
        + [pl.BlockSpec(memory_space=pltpu.VMEM)] * (1 + len(pieces))
        + [pl.BlockSpec(memory_space=pl.ANY)] * len(later),
        out_specs=[pl.BlockSpec(memory_space=pltpu.VMEM)] * waves,
        out_shape=[jax.ShapeDtypeStruct(shape, BF16)] * waves,
        scratch_shapes=[pltpu.VMEM((waves, *shape), BF16)],
        compiler_params=pltpu.CompilerParams(vmem_limit_bytes=VMEM_LIMIT),
        cost_estimate=pl.CostEstimate(flops=1, bytes_accessed=1, transcendentals=0),
        name="lens_intensity",
    )(me, wave, table, *pieces, *later)


def shifts(waves):
    return -(OFFSET // 4), (waves - 1 + OFFSET - 1 + LMAX - 1) // 4


def block_light(amounts, masks, slots, at, part, waves, reach):
    light = [[None] * 4 for _ in range(4)]
    for shift in range(reach[0], reach[1] + 1):
        rows = pl.Slice(2 * (at + MARGIN - shift), 8, 2)
        slot = slots.at[part][rows, :]
        value = [amounts.at[wave, part][rows, :] for wave in range(waves)]
        mask = [masks.at[wave, part][rows, :] for wave in range(waves)]
        picks = [slot == which for which in range(4)]
        for step in range(4):
            height = 4 * shift + step
            strip = None
            for wave in range(waves):
                if not wave - OFFSET <= height <= wave + OFFSET + LMAX - 2:
                    continue
                bit = (mask[wave] & (1 << (height + OFFSET))) != 0
                term = jnp.where(bit, value[wave], 0.0)
                strip = term if strip is None else strip + term
            if strip is None:
                continue
            for which in range(4):
                term = jnp.where(picks[which], strip, 0.0)
                held = light[step][which]
                light[step][which] = term if held is None else held + term
    return light


def put_planes(light, planes, at, part):
    for step in range(4):
        for which in range(4):
            planes.at[4 * part + which][pl.Slice(at + step, 8, 4), :] = light[step][which]


def spread(planes, out_ref, rows):
    source, target = iota((2 * LANES, 4 * LANES), 0), iota((2 * LANES, 4 * LANES), 1)
    first = jnp.where(source < LANES, 4 * source, 4 * (source - LANES) + 1)
    places = [one_hot(target == first + 2 * pair) for pair in range(2)]
    for part in range(planes.shape[0] // 4):
        value = None
        for pair, place in enumerate(places):
            at = 4 * part + 2 * pair
            plane = jnp.concatenate([planes[at, rows], planes[at + 1, rows]], axis=1)
            high = plane.astype(BF16)
            low = (plane - high.astype(F32)).astype(BF16)
            term = jnp.dot(high, place, preferred_element_type=F32)
            term = term + jnp.dot(low, place, preferred_element_type=F32)
            value = term if value is None else value + term
        out_ref[rows, part * 4 * LANES : (part + 1) * 4 * LANES] = value


def edge_kernel(starts, lengths, slot, *rest):
    up, down = rest[-2:]
    waves, block, _ = starts.shape
    for out, rows in ((up, slice(0, MARGIN)), (down, slice(block - MARGIN, block))):
        out[:waves] = starts[:, rows]
        out[waves : 2 * waves] = lengths[:, rows]
        out[2 * waves] = slot[rows]


def edge_traces(starts, lengths, slot, later):
    waves, _, columns = starts.shape
    shape = jax.ShapeDtypeStruct((2 * waves + 1, MARGIN, columns), jnp.int32)
    return pl.pallas_call(
        edge_kernel,
        in_specs=[pl.BlockSpec(memory_space=pltpu.VMEM)] * 3
        + [pl.BlockSpec(memory_space=pl.ANY)] * len(later),
        out_specs=[pl.BlockSpec(memory_space=pltpu.VMEM)] * 2,
        out_shape=[shape] * 2,
        compiler_params=pltpu.CompilerParams(vmem_limit_bytes=VMEM_LIMIT),
        cost_estimate=pl.CostEstimate(flops=1, bytes_accessed=1, transcendentals=0),
        name="edge_traces",
    )(starts, lengths, slot, *later)


def tile_kernel(waves, place_ref, *rest):
    tiles, rest = rest[:waves], rest[waves:]
    starts, lengths, slot, above, below, out_ref, amounts, masks, slots, planes = rest
    block, columns = slot.shape
    lens0 = place_ref[0] * block
    own = slice(MARGIN, block + MARGIN)
    edges = ((slice(0, MARGIN), above), (slice(block + MARGIN, block + 2 * MARGIN), below))
    every = range(columns // LANES)

    def keep(ref, rows, value):
        for part in every:
            here = pl.Slice(2 * rows.start, rows.stop - rows.start, 2)
            ref.at[part][here, :] = value[:, part * LANES : (part + 1) * LANES]

    keep(slots, own, slot[...])
    for rows, edge in edges:
        keep(slots, rows, edge[2 * waves])
    for hop in range(waves):
        which = place_ref[1] ^ hop
        tile = tiles[hop][...].astype(F32)
        parts = [(own, starts[which], lengths[which])]
        parts += [(rows, edge[which], edge[waves + which]) for rows, edge in edges]
        for rows, start, length in parts:
            lens = lens0 + rows.start - MARGIN + iota(start.shape, 0)
            amount = tile[rows] / jnp.maximum(length, 1).astype(F32)
            keep(amounts.at[which], rows, amount)
            mask = ((1 << length) - 1) << jnp.maximum(start - 4 * lens + OFFSET, 0)
            keep(masks.at[which], rows, mask)

    def body(group, _):
        at = pl.multiple_of(group * 8, 8)
        for part in range(columns // LANES):
            light = block_light(amounts, masks, slots, at, part, waves, shifts(waves))
            put_planes(light, planes, at * 4, part)
        return 0

    lax.fori_loop(0, block // 8, body, 0)
    spread(planes, out_ref, slice(0, 4 * block))


def tile_light(waves, place, tiles, starts, lengths, slot, above, below):
    block, columns = slot.shape
    high = block + 2 * MARGIN
    return pl.pallas_call(
        functools.partial(tile_kernel, waves),
        in_specs=[pl.BlockSpec(memory_space=pltpu.SMEM)]
        + [pl.BlockSpec(memory_space=pltpu.VMEM)] * (len(tiles) + 5),
        out_specs=pl.BlockSpec(memory_space=pltpu.VMEM),
        out_shape=jax.ShapeDtypeStruct((4 * block, 4 * columns), F32),
        scratch_shapes=[
            pltpu.VMEM((waves, columns // LANES, 2 * high, LANES), F32),
            pltpu.VMEM((waves, columns // LANES, 2 * high, LANES), jnp.int32),
            pltpu.VMEM((columns // LANES, 2 * high, LANES), jnp.int32),
            pltpu.VMEM((4 * columns // LANES, 4 * block, LANES), F32),
        ],
        compiler_params=pltpu.CompilerParams(vmem_limit_bytes=VMEM_LIMIT),
        cost_estimate=pl.CostEstimate(flops=1, bytes_accessed=1, transcendentals=0),
        name="tile_light",
    )(place, *tiles, starts, lengths, slot, above, below)


def exchange(pieces, axis):
    count = lax.axis_size(axis)
    received = list(pieces)
    for hop in sorted(range(1, count), key=lambda hop: ORDER.index(hop) if hop in ORDER else hop):
        pairs = [(source, source ^ hop) for source in range(count)]
        received[hop] = lax.ppermute(pieces[hop], axis, pairs)
    return received


def shifted(value, axis, steps):
    count = lax.axis_size(axis)
    initial, last = (max(0, -steps), min(count, count - steps))
    return lax.ppermute(value, axis, [(source, source + steps) for source in range(initial, last)])


def per_device(lyot_field, wave_scale, trace_start, trace_length, column_slot):
    parts, waves = lax.axis_size("row"), lax.axis_size("wave")
    block = column_slot.shape[0]
    row_index = lax.axis_index("row").astype(jnp.int32)
    wave_index = lax.axis_index("wave").astype(jnp.int32)
    me, wave = row_index.reshape(1), wave_index.reshape(1)
    place = jnp.stack([row_index, wave_index])
    halo = 4 * -(-max(shifts(waves)[1], -shifts(waves)[0]) // 4)
    layout = (((-halo, block + halo),),)
    sent = []
    for ranges in layout:
        later = [sent[-1][hop] for hop in FIRST if hop < parts] if sent else []
        pieces = half_transform(ranges, parts, block, me, wave_scale, lyot_field[0], later)
        sent.append(exchange(pieces, "row"))
    later = [sent[-1][hop] for hop in AHEAD if hop < parts]
    up, down = edge_traces(trace_start, trace_length, column_slot, later)
    above = shifted(down, "row", 1)
    below = shifted(up, "row", -1)
    table = lens_table(wave_scale, lyot_field.shape[3], [*later, up])
    later = [above, below]
    intensity = lens_intensity(layout, parts, waves, block, me, wave, table, sent, later)
    tiles = exchange(intensity, "wave")
    return tile_light(
        waves, place, tiles, trace_start, trace_length, column_slot, above, below
    )


MARGIN = 8
ROOM = 48
AHEAD = (1, 2)
ORDER = ()
WIDTH = 4096
SIZE = 512
FIRST = (0, 1, 2)


def solution(mesh):
    placed = (
        P("wave", "row", None, None),
        P("wave"),
        P(None, "row", "wave"),
        P(None, "row", "wave"),
        P("row", "wave"),
    )
    return jax.shard_map(
        per_device, mesh=mesh, in_specs=placed, out_specs=P("row", "wave"), check_vma=False
    )
```

```python
import functools
import math

import jax
import jax.numpy as jnp
from jax import lax
from jax.experimental import pallas as pl
from jax.experimental.pallas import tpu as pltpu
from jax.sharding import PartitionSpec as P

NQ = 1024
OFFSET = 8
LMAX = 8
LANES = 128
F32 = jnp.float32
BF16 = jnp.bfloat16
MIB = 1024 * 1024
VMEM_LIMIT = 20 * MIB


def iota(shape, dim):
    return lax.broadcasted_iota(jnp.int32, shape, dim)


def dot_nt(a, b):
    return lax.dot_general(a, b, (((1,), (1,)), ((), ())), preferred_element_type=F32)


def one_hot(mask):
    return jnp.where(mask, 1.0, 0.0).astype(BF16)


def cos_sin_turns(turns):
    angle = (turns - jnp.round(turns)) * math.pi
    square = angle * angle
    sine = jnp.full_like(angle, 1.0 / math.factorial(13))
    for order in (11, 9, 7, 5, 3, 1):
        sine = sine * square + (-1.0) ** ((order - 1) // 2) / math.factorial(order)
    sine = sine * angle
    cosine = jnp.full_like(angle, 1.0 / math.factorial(16))
    for order in (14, 12, 10, 8, 6, 4, 2, 0):
        cosine = cosine * square + (-1.0) ** (order // 2) / math.factorial(order)
    return 1.0 - 2.0 * sine * sine, 2.0 * sine * cosine


def count_of(ranges):
    return sum(stop - start for start, stop in ranges)


def start_turns(first, here, pupil, scale, turn, step):
    coarse = jnp.floor(scale * 4096.0) * (1.0 / 4096.0)
    fine = scale - coarse
    shape = (here.stop - here.start, LANES)
    lens = (iota(shape, 0) + first).astype(F32) - (NQ - 1) / 2.0
    place = iota(shape, 1).astype(F32) - (pupil - 1) / 2.0
    cosine, sine = cos_sin_turns(lens * place * (scale * (1.0 / pupil)))
    norm = 1.0 / math.sqrt(pupil)
    turn[0, here] = cosine * norm
    turn[1, here] = sine * norm
    whole = lens * coarse * (LANES / pupil)
    whole = whole - jnp.round(whole)
    cosine, sine = cos_sin_turns(whole + lens * fine * (LANES / pupil))
    step[0, here] = cosine
    step[1, here] = sine


def turn_table(low, high, turn, step, table):
    half = table.shape[0] // 2

    for first in range(0, half, 32):
        here = slice(first, min(first + 32, half))
        rotation = step[0, here], step[1, here]
        cosine, sine = turn[0, here], turn[1, here]
        for start in range(low, high, LANES):
            table[here, start : start + LANES] = cosine.astype(BF16)
            table[half + first : half + here.stop, start : start + LANES] = sine.astype(BF16)
            cosine, sine = (
                cosine * rotation[0] - sine * rotation[1],
                sine * rotation[0] + cosine * rotation[1],
            )
        turn[0, here] = cosine
        turn[1, here] = sine


def table_kernel(scale_ref, *rest):
    table, turn, step = rest[-3:]
    half, pupil = table.shape[0] // 2, table.shape[1]
    for low in range(0, half, 64):
        here = slice(low, min(low + 64, half))
        start_turns(low, here, pupil, scale_ref[0], turn, step)
        rotation = step[0, here], step[1, here]
        cosine, sine = turn[0, here], turn[1, here]
        for start in range(0, pupil, LANES):
            table[here, start : start + LANES] = cosine.astype(BF16)
            table[half + low : half + here.stop, start : start + LANES] = sine.astype(BF16)
            cosine, sine = (
                cosine * rotation[0] - sine * rotation[1],
                sine * rotation[0] + cosine * rotation[1],
            )


def lens_table(scale, pupil, later):
    return pl.pallas_call(
        table_kernel,
        in_specs=[pl.BlockSpec(memory_space=pltpu.SMEM)]
        + [pl.BlockSpec(memory_space=pl.ANY)] * len(later),
        out_specs=pl.BlockSpec(memory_space=pltpu.VMEM),
        out_shape=jax.ShapeDtypeStruct((NQ, pupil), BF16),
        scratch_shapes=[pltpu.VMEM((2, NQ // 2, LANES), F32)] * 2,
        compiler_params=pltpu.CompilerParams(vmem_limit_bytes=VMEM_LIMIT),
        cost_estimate=pl.CostEstimate(flops=1, bytes_accessed=1, transcendentals=0),
        name="lens_table",
    )(scale, *later)


def half_kernel(ranges, parts, block, width, size, extra, me_ref, scale_ref, field_hbm, *rest):
    outs = rest[extra : extra + parts]
    field, table, turn, step, halves, arrived = rest[extra + parts :]
    samples, _, pupil = field_hbm.shape
    half = table.shape[0] // 2
    rows = count_of(ranges)
    loads = {}
    for piece in range(samples // size):
        for low in range(0, pupil, width):
            here = (pl.ds(piece * size, size), slice(None), pl.ds(low, width))
            loads[piece, low] = pltpu.make_async_copy(
                field_hbm.at[here], field.at[here], arrived.at[len(loads)]
            )
            loads[piece, low].start()

    at = 0
    for group in range(parts // 2):
        for low, high in ranges:
            here = slice(at, at + high - low)
            start_turns(group * block + low, here, pupil, scale_ref[0], turn, step)
            at += high - low
    source, target = iota((2 * LANES, 2 * LANES), 0), iota((2 * LANES, 2 * LANES), 1)
    apart = one_hot(source == jnp.where(target < LANES, 2 * target, 2 * (target - LANES) + 1))
    for piece in range(samples // size):
        product = None
        for low in range(0, pupil, width):
            lanes = slice(low, low + width)
            if piece == 0:
                turn_table(low, low + width, turn, step, table)
            loads[piece, low].wait()
            here = field[piece * size : (piece + 1) * size, :, lanes].reshape(2 * size, width)
            term = dot_nt(table[:, lanes], here)
            product = term if product is None else product + term
        for inner in range(size // LANES):
            even_odd = []
            for side in range(2):
                lanes = slice((2 * inner + side) * LANES, (2 * inner + side + 1) * LANES)
                direct, cross = product[:half, lanes], product[half:, lanes]
                swapped = jnp.where(
                    iota(cross.shape, 1) % 2 == 0,
                    pltpu.roll(cross, LANES - 1, 1),
                    -pltpu.roll(cross, 1, 1),
                )
                even_odd.append((direct + swapped, direct - swapped))
            first = piece * size + inner * LANES
            lanes = slice(first, first + LANES)
            for mirrored in range(2):
                both = jnp.concatenate([pair[mirrored] for pair in even_odd], axis=1)
                both = jnp.dot(both.astype(BF16), apart, preferred_element_type=F32)
                for group in range(parts // 2):
                    owner = parts - 1 - group if mirrored else group
                    here = slice(group * rows, (group + 1) * rows)
                    halves[owner, :rows, lanes] = both[here, :LANES].astype(BF16)
                    halves[owner, rows:, lanes] = both[here, LANES:].astype(BF16)
    for hop in range(parts):
        outs[hop][...] = halves[me_ref[0] ^ hop]


def half_transform(ranges, parts, block, me, scale, field, later):
    samples, _, pupil = field.shape
    rows = count_of(ranges)
    height = parts * rows
    width, size = min(WIDTH, pupil), min(SIZE, samples)
    return pl.pallas_call(
        functools.partial(half_kernel, ranges, parts, block, width, size, len(later)),
        in_specs=[pl.BlockSpec(memory_space=pltpu.SMEM)] * 2
        + [pl.BlockSpec(memory_space=pl.ANY)] * (1 + len(later)),
        out_specs=[pl.BlockSpec(memory_space=pltpu.VMEM)] * parts,
        scratch_shapes=[
            pltpu.VMEM(field.shape, BF16),
            pltpu.VMEM((height, pupil), BF16),
            pltpu.VMEM((2, height // 2, LANES), F32),
            pltpu.VMEM((2, height // 2, LANES), F32),
            pltpu.VMEM((parts, 2 * rows, samples), BF16),
            pltpu.SemaphoreType.DMA((pupil // width * (samples // size),)),
        ],
        out_shape=[jax.ShapeDtypeStruct((2 * rows, samples), BF16)] * parts,
        compiler_params=pltpu.CompilerParams(vmem_limit_bytes=ROOM * MIB),
        cost_estimate=pl.CostEstimate(flops=1, bytes_accessed=1, transcendentals=0),
        name="half_transform",
    )(me, scale, field, *later)


def lens_kernel(layout, parts, waves, block, extra, me_ref, wave_ref, table, *rest):
    kinds = len(layout)
    pieces, rest = rest[: kinds * parts], rest[kinds * parts :]
    outs, tiles = rest[extra : extra + waves], rest[extra + waves]
    me, wave = me_ref[0], wave_ref[0]
    half = table.shape[0] // 2
    samples = pieces[0].shape[1]
    total = None
    for hop in range(parts):
        near = [pieces[kind * parts + hop][...] for kind in range(kinds)]
        lanes = pl.ds(pl.multiple_of((me ^ hop) * samples, samples), samples)
        term = dot_nt(jnp.concatenate(near, axis=0), table[:, lanes])
        total = term if hop == 0 else total + term

    strips, spans, at = ([], []), [], 0
    for ranges in layout:
        rows = count_of(ranges)
        real, imag = total[at : at + rows], total[at + rows : at + 2 * rows]
        at += 2 * rows
        for mirrored, sign in enumerate((1.0, -1.0)):
            lens_real = real[:, :half] + sign * imag[:, half:]
            lens_imag = imag[:, :half] - sign * real[:, half:]
            strips[mirrored].append(lens_real * lens_real + lens_imag * lens_imag)
        spans.extend(ranges)
    height, columns = tiles.shape[1:]
    count = sum(count_of(ranges) for ranges in layout)
    held = iota((height, count), 1)
    row, at = jnp.zeros((height, count), jnp.int32), 0
    for low, high in spans:
        row = jnp.where(held >= at, held - at + low, row)
        at += high - low
    row = jnp.where(me >= parts // 2, block - 1 - row, row)
    pick = one_hot(row == iota((height, count), 0) - MARGIN)
    back = one_hot(iota((columns, columns), 0) == columns - 1 - iota((columns, columns), 1))
    for mirrored in range(2):
        strip = jnp.concatenate(strips[mirrored], axis=0).astype(BF16)
        strip = jnp.dot(pick, strip, preferred_element_type=F32).astype(BF16)
        for group in range(waves // 2):
            tile = strip[:, group * columns : (group + 1) * columns]
            if mirrored:
                tile = jnp.dot(tile, back, preferred_element_type=F32).astype(BF16)
            tiles[waves - 1 - group if mirrored else group] = tile
    for hop in range(waves):
        outs[hop][...] = tiles[wave ^ hop]


def lens_intensity(layout, parts, waves, block, me, wave, table, sent, later):
    shape = (block + 2 * MARGIN, NQ // waves)
    pieces = [piece for part in sent for piece in part]
    return pl.pallas_call(
        functools.partial(lens_kernel, layout, parts, waves, block, len(later)),
        in_specs=[pl.BlockSpec(memory_space=pltpu.SMEM)] * 2
        + [pl.BlockSpec(memory_space=pltpu.VMEM)] * (1 + len(pieces))
        + [pl.BlockSpec(memory_space=pl.ANY)] * len(later),
        out_specs=[pl.BlockSpec(memory_space=pltpu.VMEM)] * waves,
        out_shape=[jax.ShapeDtypeStruct(shape, BF16)] * waves,
        scratch_shapes=[pltpu.VMEM((waves, *shape), BF16)],
        compiler_params=pltpu.CompilerParams(vmem_limit_bytes=VMEM_LIMIT),
        cost_estimate=pl.CostEstimate(flops=1, bytes_accessed=1, transcendentals=0),
        name="lens_intensity",
    )(me, wave, table, *pieces, *later)


def shifts(waves):
    return -(OFFSET // 4), (waves - 1 + OFFSET - 1 + LMAX - 1) // 4


def block_light(amounts, masks, slots, at, part, waves, reach):
    light = [[None] * 4 for _ in range(4)]
    for shift in range(reach[0], reach[1] + 1):
        rows = pl.Slice(2 * (at + MARGIN - shift), 8, 2)
        slot = slots.at[part][rows, :]
        value = [amounts.at[wave, part][rows, :] for wave in range(waves)]
        mask = [masks.at[wave, part][rows, :] for wave in range(waves)]
        picks = [slot == which for which in range(4)]
        for step in range(4):
            height = 4 * shift + step
            strip = None
            for wave in range(waves):
                if not wave - OFFSET <= height <= wave + OFFSET + LMAX - 2:
                    continue
                bit = (mask[wave] & (1 << (height + OFFSET))) != 0
                term = jnp.where(bit, value[wave], 0.0)
                strip = term if strip is None else strip + term
            if strip is None:
                continue
            for which in range(4):
                term = jnp.where(picks[which], strip, 0.0)
                held = light[step][which]
                light[step][which] = term if held is None else held + term
    return light


def put_planes(light, planes, at, part):
    for step in range(4):
        for which in range(4):
            planes.at[4 * part + which][pl.Slice(at + step, 8, 4), :] = light[step][which]


def spread(planes, out_ref, rows):
    source, target = iota((2 * LANES, 4 * LANES), 0), iota((2 * LANES, 4 * LANES), 1)
    first = jnp.where(source < LANES, 4 * source, 4 * (source - LANES) + 1)
    places = [one_hot(target == first + 2 * pair) for pair in range(2)]
    for part in range(planes.shape[0] // 4):
        value = None
        for pair, place in enumerate(places):
            at = 4 * part + 2 * pair
            plane = jnp.concatenate([planes[at, rows], planes[at + 1, rows]], axis=1)
            high = plane.astype(BF16)
            low = (plane - high.astype(F32)).astype(BF16)
            term = jnp.dot(high, place, preferred_element_type=F32)
            term = term + jnp.dot(low, place, preferred_element_type=F32)
            value = term if value is None else value + term
        out_ref[rows, part * 4 * LANES : (part + 1) * 4 * LANES] = value


def edge_kernel(starts, lengths, slot, *rest):
    up, down = rest[-2:]
    waves, block, _ = starts.shape
    for out, rows in ((up, slice(0, MARGIN)), (down, slice(block - MARGIN, block))):
        out[:waves] = starts[:, rows]
        out[waves : 2 * waves] = lengths[:, rows]
        out[2 * waves] = slot[rows]


def edge_traces(starts, lengths, slot, later):
    waves, _, columns = starts.shape
    shape = jax.ShapeDtypeStruct((2 * waves + 1, MARGIN, columns), jnp.int32)
    return pl.pallas_call(
        edge_kernel,
        in_specs=[pl.BlockSpec(memory_space=pltpu.VMEM)] * 3
        + [pl.BlockSpec(memory_space=pl.ANY)] * len(later),
        out_specs=[pl.BlockSpec(memory_space=pltpu.VMEM)] * 2,
        out_shape=[shape] * 2,
        compiler_params=pltpu.CompilerParams(vmem_limit_bytes=VMEM_LIMIT),
        cost_estimate=pl.CostEstimate(flops=1, bytes_accessed=1, transcendentals=0),
        name="edge_traces",
    )(starts, lengths, slot, *later)


def tile_kernel(waves, place_ref, *rest):
    tiles, rest = rest[:waves], rest[waves:]
    starts, lengths, slot, above, below, out_ref, amounts, masks, slots, planes = rest
    block, columns = slot.shape
    lens0 = place_ref[0] * block
    own = slice(MARGIN, block + MARGIN)
    edges = ((slice(0, MARGIN), above), (slice(block + MARGIN, block + 2 * MARGIN), below))
    every = range(columns // LANES)

    def keep(ref, rows, value):
        for part in every:
            here = pl.Slice(2 * rows.start, rows.stop - rows.start, 2)
            ref.at[part][here, :] = value[:, part * LANES : (part + 1) * LANES]

    keep(slots, own, slot[...])
    for rows, edge in edges:
        keep(slots, rows, edge[2 * waves])
    for hop in range(waves):
        which = place_ref[1] ^ hop
        tile = tiles[hop][...].astype(F32)
        parts = [(own, starts[which], lengths[which])]
        parts += [(rows, edge[which], edge[waves + which]) for rows, edge in edges]
        for rows, start, length in parts:
            lens = lens0 + rows.start - MARGIN + iota(start.shape, 0)
            amount = tile[rows] / jnp.maximum(length, 1).astype(F32)
            keep(amounts.at[which], rows, amount)
            mask = ((1 << length) - 1) << jnp.maximum(start - 4 * lens + OFFSET, 0)
            keep(masks.at[which], rows, mask)

    def body(group, _):
        at = pl.multiple_of(group * 8, 8)
        for part in range(columns // LANES):
            light = block_light(amounts, masks, slots, at, part, waves, shifts(waves))
            put_planes(light, planes, at * 4, part)
        return 0

    lax.fori_loop(0, block // 8, body, 0)
    spread(planes, out_ref, slice(0, 4 * block))


def tile_light(waves, place, tiles, starts, lengths, slot, above, below):
    block, columns = slot.shape
    high = block + 2 * MARGIN
    return pl.pallas_call(
        functools.partial(tile_kernel, waves),
        in_specs=[pl.BlockSpec(memory_space=pltpu.SMEM)]
        + [pl.BlockSpec(memory_space=pltpu.VMEM)] * (len(tiles) + 5),
        out_specs=pl.BlockSpec(memory_space=pltpu.VMEM),
        out_shape=jax.ShapeDtypeStruct((4 * block, 4 * columns), F32),
        scratch_shapes=[
            pltpu.VMEM((waves, columns // LANES, 2 * high, LANES), F32),
            pltpu.VMEM((waves, columns // LANES, 2 * high, LANES), jnp.int32),
            pltpu.VMEM((columns // LANES, 2 * high, LANES), jnp.int32),
            pltpu.VMEM((4 * columns // LANES, 4 * block, LANES), F32),
        ],
        compiler_params=pltpu.CompilerParams(vmem_limit_bytes=VMEM_LIMIT),
        cost_estimate=pl.CostEstimate(flops=1, bytes_accessed=1, transcendentals=0),
        name="tile_light",
    )(place, *tiles, starts, lengths, slot, above, below)


def exchange(pieces, axis):
    count = lax.axis_size(axis)
    received = list(pieces)
    for hop in sorted(range(1, count), key=lambda hop: ORDER.index(hop) if hop in ORDER else hop):
        pairs = [(source, source ^ hop) for source in range(count)]
        received[hop] = lax.ppermute(pieces[hop], axis, pairs)
    return received


def shifted(value, axis, steps):
    count = lax.axis_size(axis)
    initial, last = (max(0, -steps), min(count, count - steps))
    return lax.ppermute(value, axis, [(source, source + steps) for source in range(initial, last)])


def per_device(lyot_field, wave_scale, trace_start, trace_length, column_slot):
    parts, waves = lax.axis_size("row"), lax.axis_size("wave")
    block = column_slot.shape[0]
    row_index = lax.axis_index("row").astype(jnp.int32)
    wave_index = lax.axis_index("wave").astype(jnp.int32)
    me, wave = row_index.reshape(1), wave_index.reshape(1)
    place = jnp.stack([row_index, wave_index])
    halo = 4 * -(-max(shifts(waves)[1], -shifts(waves)[0]) // 4)
    layout = (((-halo, block + halo),),)
    sent = []
    for ranges in layout:
        later = [sent[-1][hop] for hop in FIRST if hop < parts] if sent else []
        pieces = half_transform(ranges, parts, block, me, wave_scale, lyot_field[0], later)
        sent.append(exchange(pieces, "row"))
    later = [sent[-1][hop] for hop in AHEAD if hop < parts]
    up, down = edge_traces(trace_start, trace_length, column_slot, later)
    above = shifted(down, "row", 1)
    below = shifted(up, "row", -1)
    table = lens_table(wave_scale, lyot_field.shape[3], [*later, up])
    later = [above, below]
    intensity = lens_intensity(layout, parts, waves, block, me, wave, table, sent, later)
    tiles = exchange(intensity, "wave")
    return tile_light(
        waves, place, tiles, trace_start, trace_length, column_slot, above, below
    )


MARGIN = 8
ROOM = 48
AHEAD = (1, 2)
ORDER = ()
WIDTH = 4096
SIZE = 512
FIRST = (0, 1, 2)


def solution(mesh):
    placed = (
        P("wave", "row", None, None),
        P("wave"),
        P(None, "row", "wave"),
        P(None, "row", "wave"),
        P("row", "wave"),
    )
    return jax.shard_map(
        per_device, mesh=mesh, in_specs=placed, out_specs=P("row", "wave"), check_vma=False
    )
```
